32 devices in a mesh: dom: 8 (over z, x), col: 4 (over y, core).
Axes of the slice: x: 2, y: 2, z: 4, core: 2. Of those that a mesh axis runs over, the one named last changes fastest.
Arguments:
- a_vals: bfloat16 [512, 96, 864], P('dom', 'col'), may hold values from -0.625 to 0.625
- p_vals: bfloat16 [512, 96, 288], P('dom', 'col'), may hold values from -0.625 to 0.625
- a_cols: int32 [512, 9], P('dom'), may hold values from 0 to 511, as said below
- p_aggs: int32 [512, 3], replicated, may hold values from 0 to 31, as said below
- halo_rows: int32 [8, 2, 32], replicated, may hold values from 0 to 63, as said below
- live_rows: int32 [8], P('dom'), may hold values from 16 to 64, as said below
Outputs:
- galerkin: bfloat16 [3072, 1920], P(('dom', 'col'))
The draws below stay inside these ranges and needn't reach their ends.
Inputs may be any that keep to these rules, and one draw needn't show every extreme that they name: `a_cols`: row i of partition d = i div 64 holds i in slot 0 and global row numbers of partition d (d * 64 to (d + 1) * 64 - 1) in slots 1 to 4; slots 5 to 8 hold positions 0 to 31. halo_rows[d, e] holds 32 different local row numbers (0 to 63) of partition d in increasing order; where the neighbour exists, every position of the list is named by some row of it. `p_aggs`: the three ids of a row of partition d differ; the first two lie in d * 4 to (d + 1) * 4 - 1, the third in the range of partition d + 1 (of partition d for the last one). `live_rows`: at least one partition has all 64 rows live.
All inputs are finite; a program needn't handle non-finite values.
Results may differ from the reference program's by a relative error of at most 0.005.
Values may be sent and summed in bfloat16 or wider, within the bound.
No kernel may reach another device: no remote copies, remote signals or barrier semaphores. Data moves between devices by JAX's collectives and lax.ppermute only.
A program may use at most 256 MiB of HBM per device.

```python
import jax
import jax.numpy as jnp
from jax import lax

BW = 96
BC = 96
KA = 9
KP = 3
NAG = 4
NB = 64
NS = 32
NBT = 512
N_DOM = 8


def draw_halo_rows(key, part):
    parts = NBT // NB
    scores = jax.random.randint(jax.random.fold_in(key, 101), (parts, 2, NB), 0, 1 << 20)
    scores = scores * NB + jnp.arange(NB, dtype=jnp.int32)
    order = jnp.argsort(scores, axis=-1)
    return jnp.sort(order[:, :, :NS], axis=-1).astype(jnp.int32)


def draw_a_cols(key, part):
    key = jax.random.fold_in(key, 7)
    parts = NBT // NB
    which = jnp.arange(parts, dtype=jnp.int32)[:, None]
    row = jnp.arange(NB, dtype=jnp.int32)[None, :]
    own = jax.random.randint(key, (parts, NB, KA), 0, NB).astype(jnp.int32) + which[:, :, None] * NB
    slots = [which * NB + row, own[:, :, 1], own[:, :, 2], own[:, :, 3], own[:, :, 4]]
    for extra in range(4):
        spot = (2 * jnp.arange(NB, dtype=jnp.int32) + extra % 2) % NS
        slots.append(jnp.broadcast_to(spot[None, :], (parts, NB)))
    return jnp.stack(slots, axis=2).reshape(NBT, KA).astype(jnp.int32)


def draw_p_aggs(key, part):
    key = jax.random.fold_in(key, 11)
    parts = NBT // NB
    which = jnp.arange(parts, dtype=jnp.int32)[:, None]
    scores = jax.random.randint(key, (parts, NB, NAG), 0, 1 << 20)
    scores = scores * NAG + jnp.arange(NAG, dtype=jnp.int32)
    order = jnp.argsort(scores, axis=-1).astype(jnp.int32)
    first = which * NAG + order[:, :, 0]
    second = which * NAG + order[:, :, 1]
    third = jnp.where(which < parts - 1, (which + 1) * NAG + order[:, :, 2], which * NAG + order[:, :, 2])
    return jnp.stack([first, second, third], axis=2).reshape(NBT, KP).astype(jnp.int32)


def draw_live_rows(key, part):
    key = jax.random.fold_in(key, 13)
    parts = NBT // NB
    counts = jax.random.randint(key, (parts,), NB // 4, NB + 1).astype(jnp.int32)
    busiest = jax.random.randint(jax.random.fold_in(key, 1), (), 0, parts)
    return jnp.where(jnp.arange(parts, dtype=jnp.int32) == busiest, NB, counts).astype(jnp.int32)


def block_levels(rng, extent, cuts, low, largest):
    factor_of, own = 1.0, jax.random.fold_in(rng, 6)
    for axis_at, blocks in cuts:
        heights = jnp.exp(jax.random.uniform(jax.random.fold_in(own, axis_at), (blocks,), jnp.float32, low / len(cuts), largest / len(cuts)))
        factor_of = factor_of * jnp.repeat(heights, extent[axis_at] // blocks).reshape([-1 if axis == axis_at else 1 for axis in range(len(extent))])
    return factor_of


def gaussian(key, shape, scale, most, split=(), kind=jnp.bfloat16):
    values = jax.random.normal(key, shape, jnp.float32) * scale
    if len(split) > 0:
        values = block_levels(key, shape, split, -0.22, 0.18) * values
    return jnp.clip(values, min=-most, max=most).astype(kind)


def setup_inputs(seed: int = 0) -> dict:
    arg_keys = jax.random.split(jax.random.key(seed), 7)
    a_vals = gaussian(arg_keys[0], (NBT, BW, KA * BW), BW ** -0.5, 0.625, ((0, 8), (1, 4)))
    p_vals = gaussian(arg_keys[1], (NBT, BW, KP * BC), BW ** -0.5, 0.625, ((0, 8), (1, 4)))
    a_cols = draw_a_cols(jax.random.fold_in(arg_keys[6], 71), 0)
    p_aggs = draw_p_aggs(jax.random.fold_in(arg_keys[6], 71), 0)
    halo_rows = draw_halo_rows(jax.random.fold_in(arg_keys[6], 71), 0)
    live_rows = draw_live_rows(jax.random.fold_in(arg_keys[6], 71), 0)
    return dict(a_vals=a_vals, p_vals=p_vals, a_cols=a_cols, p_aggs=p_aggs, halo_rows=halo_rows, live_rows=live_rows)


HIGH = lax.Precision.HIGHEST


def resolve_columns(part, a_cols, halo_rows):
    cols = lax.dynamic_slice_in_dim(a_cols, part * NB, NB, 0)
    lower_list = halo_rows[jnp.maximum(part - 1, 0), 1]
    upper_list = halo_rows[jnp.minimum(part + 1, N_DOM - 1), 0]
    q_low = cols[:, 5:7]
    q_up = cols[:, 7:9]
    low_res = jnp.where(part > 0, (part - 1) * NB + jnp.take(lower_list, q_low, axis=0), part * NB + q_low)
    up_res = jnp.where(part < N_DOM - 1, (part + 1) * NB + jnp.take(upper_list, q_up, axis=0), part * NB + q_up)
    return jnp.concatenate([cols[:, :5], low_res, up_res], axis=1).astype(jnp.int32)


def partition_terms(part, a_vals, p_vals, a_cols, p_aggs, halo_rows, live_rows):
    start = part * NB
    a_part = lax.dynamic_slice_in_dim(a_vals, start, NB, 0)
    cols = resolve_columns(part, a_cols, halo_rows)
    own_p = lax.dynamic_slice_in_dim(p_vals, start, NB, 0)
    own_aggs = lax.dynamic_slice_in_dim(p_aggs, start, NB, 0) - part * NAG
    products = []
    for slot in range(KA):
        block = a_part[:, :, slot * BW:(slot + 1) * BW].astype(jnp.float32)
        fetched = jnp.take(p_vals, cols[:, slot], axis=0).astype(jnp.float32)
        products.append(jnp.einsum("iwv,ivx->iwx", block, fetched, precision=HIGH))
    stacked = jnp.stack(products, axis=2).reshape(NB, BW, KA * KP, BC)
    used = jnp.take(p_aggs, cols, axis=0).reshape(NB, KA * KP) - (part - 1) * NAG
    select = (used[:, :, None] == jnp.arange(4 * NAG, dtype=jnp.int32)[None, None, :]).astype(jnp.float32)
    coupled = jnp.einsum("iwsc,isj->iwjc", stacked, select, precision=HIGH)
    coupled = coupled.reshape(NB, BW, 4 * NAG * BC).astype(jnp.bfloat16)
    live = (jnp.arange(NB, dtype=jnp.int32) < live_rows[part]).astype(jnp.float32)
    pick = (own_aggs[:, :, None] == jnp.arange(2 * NAG, dtype=jnp.int32)[None, None, :]).astype(jnp.float32)
    pick = pick * live[:, None, None]
    spread = jnp.einsum("iwmc,imj->iwjc", own_p.reshape(NB, BW, KP, BC).astype(jnp.float32), pick, precision=HIGH)
    spread = spread.reshape(NB, BW, 2 * NAG * BC)
    return jnp.einsum("iwa,iwx->ax", spread, coupled.astype(jnp.float32), precision=HIGH)


def reference(a_vals, p_vals, a_cols, p_aggs, halo_rows, live_rows):
    partials = lax.map(lambda part: partition_terms(part, a_vals, p_vals, a_cols, p_aggs, halo_rows, live_rows),
                       jnp.arange(N_DOM, dtype=jnp.int32))
    band = NAG * BC
    result = jnp.zeros((N_DOM, band, 5 * band), jnp.float32)
    result = result.at[:, :, band:].add(partials[:, :band, :])
    result = result.at[1:, :, :4 * band].add(partials[:-1, band:, :])
    return result.reshape(N_DOM * band, 5 * band).astype(jnp.bfloat16)
```

```python
import jax
import jax.numpy as jnp
from jax import lax
from jax.experimental import pallas as pl
from jax.experimental.pallas import tpu as pltpu
from jax.sharding import PartitionSpec as P

BW = 96
BC = 96
KA = 9
KP = 3
NAG = 4
NB = 64
NS = 32
W = 24
ROWS = NB * W
AXES = ("dom", "col")
VMEM_LIMIT = 56 * 1024 * 1024
F32, BF16 = jnp.float32, jnp.bfloat16


def params():
    return pltpu.CompilerParams(vmem_limit_bytes=VMEM_LIMIT)


def whole_vmem():
    return pl.BlockSpec(memory_space=pltpu.VMEM)


def smem():
    return pl.BlockSpec(memory_space=pltpu.SMEM)


def anywhere():
    return pl.BlockSpec(memory_space=pl.ANY)


def pack_own_kernel(p_ref, out_ref):
    out_ref[0:ROWS, :] = p_ref[:, 0:256]
    for g in range(NB // 16):
        tails = [p_ref[48 * (8 * g + q) : 48 * (8 * g + q) + 48, 256:288] for q in range(8)]
        out_ref[ROWS + 48 * g : ROWS + 48 * g + 48, :] = jnp.concatenate(tails, axis=1)


def pack_halo_kernel(lists_ref, p_ref, down_ref, up_ref, wide_ref):
    def widen(t, carry):
        pair = p_ref[pl.ds(pl.multiple_of(t * 48, 48), 48), :].astype(F32)
        wide_ref[2 * t] = pair[0:24]
        wide_ref[2 * t + 1] = pair[24:48]
        return carry

    lax.fori_loop(0, NB // 2, widen, 0)
    for e, out_ref in ((0, down_ref), (1, up_ref)):
        for g in range(NS // 16):
            tails = []
            for q in range(8):
                t = 8 * g + q
                first = wide_ref[lists_ref[e * NS + 2 * t]]
                second = wide_ref[lists_ref[e * NS + 2 * t + 1]]
                pair = jnp.concatenate([first, second], axis=0).astype(BF16)
                out_ref[48 * t : 48 * t + 48, :] = pair[:, 0:256]
                tails.append(pair[:, 256:288])
            start = NS * W + 48 * g
            out_ref[start : start + 48, :] = jnp.concatenate(tails, axis=1)


def spread_kernel(p_ref, mask_ref, out_ref):
    eye = (
        lax.broadcasted_iota(jnp.int32, (288, 288), 0)
        == lax.broadcasted_iota(jnp.int32, (288, 288), 1)
    ).astype(F32).astype(BF16)
    for n in range(3):
        cols = slice(512 * n, 512 * n + 512)
        flipped = lax.dot_general(
            eye, p_ref[cols, :], (((1,), (1,)), ((), ())), preferred_element_type=F32
        )
        for b in range(8):
            total = jnp.zeros((BC, 512), F32)
            for m in range(KP):
                row = mask_ref[3 * b + m : 3 * b + m + 1, cols]
                total += flipped[BC * m : BC * m + BC] * row
            out_ref[BC * b : BC * b + BC, cols] = total.astype(BF16)


def unpack(count, agg_of, sources_ref, blocks_ref):
    blocks_ref[...] = jnp.zeros_like(blocks_ref)
    lane = lax.broadcasted_iota(jnp.int32, (48, 128), 1)

    def group(g, carry):
        for q in range(8):
            t = 8 * g + q
            parts = [[], [], []]
            for v in range(4):
                rows = pl.ds(pl.multiple_of(t * 48, 48), 48)
                x0 = sources_ref[v, rows, 0:128].astype(F32)
                x1 = sources_ref[v, rows, 128:256].astype(F32)
                tail_rows = pl.ds(pl.multiple_of(count * W + g * 48, 48), 48)
                half = 128 * (q // 4)
                tail = sources_ref[v, tail_rows, half : half + 128].astype(F32)
                shift = (64 - 32 * (q % 4)) % 128
                if shift:
                    tail = pltpu.roll(tail, shift, 1)
                parts[0].append(x0)
                parts[1].append(
                    jnp.where(lane < 32, pltpu.roll(x0, 32, 1), pltpu.roll(x1, 32, 1))
                )
                parts[2].append(jnp.where(lane < 64, pltpu.roll(x1, 64, 1), tail))
            for j in range(KP):
                for odd in range(2):
                    r = 2 * t + odd
                    block = jnp.concatenate([x[24 * odd : 24 * odd + 24] for x in parts[j]], axis=0)
                    at = pl.multiple_of(agg_of(r, j) * 128, 128)
                    blocks_ref[r, :, pl.ds(at, 128)] = block.astype(BF16)
        return carry

    lax.fori_loop(0, count // 16, group, 0)


def fetch(refs, scratch, sems, col):
    copies = [
        pltpu.make_async_copy(ref, scratch.at[jnp.bitwise_xor(col, s)], sems.at[s])
        for s, ref in enumerate(refs)
    ]
    for copy in copies:
        copy.start()
    for copy in copies:
        copy.wait()


def own_kernel(place_ref, cols_ref, aggs_ref, s0, s1, s2, s3, a_ref, low_ref, up_ref, below_ref, above_ref,
               sources, blocks, sems):
    col, first, last = place_ref[0], place_ref[1], place_ref[2]
    fetch((s0, s1, s2, s3), sources, sems, col)
    unpack(NB, lambda r, j: aggs_ref[KP * r + j], sources, blocks)
    pad32 = jnp.zeros((32, 1024), BF16)
    pad64 = jnp.zeros((64, 1024), BF16)

    def pair(t, carry):
        rows = pl.ds(pl.multiple_of(t * 48, 48), 48)
        a = a_ref[rows, 0:512]
        done = []
        for odd in range(2):
            at = KA * (2 * t + odd)
            weights = jnp.concatenate([blocks[cols_ref[at + k]] for k in range(5)] + [pad32], axis=0)
            got = jnp.dot(a[16 * odd : 16 * odd + 32], weights, preferred_element_type=F32)
            done.append(got[8 * odd : 8 * odd + 24])
        total = jnp.concatenate(done, axis=0)
        below_ref[rows, :] = total[:, 0:512]
        above_ref[rows, :] = total[:, 512:1024]
        return carry

    lax.fori_loop(0, NB // 2, pair, 0)

    def edge(a_edge, slot, order):
        def pair(t, carry):
            rows = pl.ds(pl.multiple_of(t * 48, 48), 48)
            a = a_edge[rows, :]
            done = []
            for odd in range(2):
                at = KA * (2 * t + odd) + slot
                pieces = [blocks[cols_ref[at]], blocks[cols_ref[at + 1]]]
                weights = jnp.concatenate(order(pieces, pad64), axis=0)
                got = jnp.dot(a[16 * odd : 16 * odd + 32], weights, preferred_element_type=F32)
                done.append(got[8 * odd : 8 * odd + 24])
            total = jnp.concatenate(done, axis=0)
            below_ref[rows, :] += total[:, 0:512]
            above_ref[rows, :] += total[:, 512:1024]
            return carry

        lax.fori_loop(0, NB // 2, pair, 0)

    @pl.when(first == 1)
    def _():
        edge(low_ref, 5, lambda pieces, pad: pieces + [pad])

    @pl.when(last == 1)
    def _():
        edge(up_ref, 7, lambda pieces, pad: [pad] + pieces)


def make_halo_kernel(upper):
    def kernel(place_ref, cols_ref, list_ref, aggs_ref, s0, s1, s2, s3, a_ref, own_ref, spread_ref,
               send_ref, keep_ref, sources, blocks, coupled, sems):
        fetch((s0, s1, s2, s3), sources, sems, place_ref[0])
        unpack(NS, lambda r, j: aggs_ref[KP * list_ref[r] + j], sources, blocks)
        pad64 = jnp.zeros((64, 1024), BF16)

        def pair(t, carry):
            rows = pl.ds(pl.multiple_of(t * 48, 48), 48)
            a = a_ref[rows, :]
            own = own_ref[rows, :]
            done = []
            for odd in range(2):
                at = KA * (2 * t + odd) + (7 if upper else 5)
                pieces = [blocks[cols_ref[at]], blocks[cols_ref[at + 1]]]
                pieces = [pad64] + pieces if upper else pieces + [pad64]
                weights = jnp.concatenate(pieces, axis=0)
                got = jnp.dot(a[16 * odd : 16 * odd + 32], weights, preferred_element_type=F32)
                done.append(got[8 * odd : 8 * odd + 24])
            total = jnp.concatenate(done, axis=0)
            if upper:
                total = jnp.concatenate([total[:, 0:512] + own, total[:, 512:1024]], axis=1)
            else:
                total = jnp.concatenate([total[:, 0:512], total[:, 512:1024] + own], axis=1)
            coupled[rows, :] = total.astype(BF16)
            return carry

        lax.fori_loop(0, NB // 2, pair, 0)
        lane = lax.broadcasted_iota(jnp.int32, (128, 128), 1)
        for n in range(2):
            for half, out_ref in ((0, send_ref), (1, keep_ref)):
                def tile(m, carry):
                    rows = pl.ds(pl.multiple_of(m * 128, 128), 128)
                    from_rows = pl.ds(pl.multiple_of(384 * half + m * 128, 128), 128)
                    y = jnp.dot(
                        spread_ref[from_rows, :],
                        coupled[:, 512 * n : 512 * n + 512],
                        preferred_element_type=F32,
                    )
                    y0, y1, y2, y3 = [y[:, 128 * c : 128 * c + 128] for c in range(4)]
                    y1, y2, y3 = pltpu.roll(y1, 96, 1), pltpu.roll(y2, 64, 1), pltpu.roll(y3, 32, 1)
                    packed = [
                        jnp.where(lane < 96, y0, y1),
                        jnp.where(lane < 64, y1, y2),
                        jnp.where(lane < 32, y2, y3),
                    ]
                    for c in range(3):
                        at = 384 * n + 128 * c
                        out_ref[rows, at : at + 128] = packed[c].astype(out_ref.dtype)
                    return carry

                lax.fori_loop(0, 3, tile, 0)

    return kernel


def local(a_vals, p_vals, a_cols, p_aggs, halo_rows, live_rows):
    part = lax.axis_index("dom")
    parts = lax.axis_size("dom")
    col = lax.axis_index("col")
    cols_count = lax.axis_size("col")
    devices = [(d, c) for d in range(parts) for c in range(cols_count)]

    def moved(x, step, flip):
        route = [
            (d * cols_count + c, (d + step) * cols_count + (c ^ flip))
            for d, c in devices
            if 0 <= d + step < parts
        ]
        return lax.ppermute(x, AXES, route)

    p_flat = p_vals.reshape(ROWS, KP * BC)
    a_flat = a_vals.reshape(ROWS, KA * BW)

    own_pack = pl.pallas_call(
        pack_own_kernel,
        out_shape=jax.ShapeDtypeStruct((ROWS + 192, 256), BF16),
        in_specs=[whole_vmem()],
        out_specs=whole_vmem(),
        compiler_params=params(),
    )(p_flat)
    lists = lax.dynamic_slice_in_dim(halo_rows, part, 1, 0).reshape(2 * NS)
    halo_shape = jax.ShapeDtypeStruct((NS * W + 96, 256), BF16)
    down_pack, up_pack = pl.pallas_call(
        pack_halo_kernel,
        out_shape=[halo_shape, halo_shape],
        in_specs=[smem(), whole_vmem()],
        out_specs=[whole_vmem(), whole_vmem()],
        scratch_shapes=[pltpu.VMEM((NB, W, KP * BC), F32)],
        compiler_params=params(),
    )(lists, p_flat)

    def gathered(x):
        near = moved(x, 0, 2)
        return (x, moved(x, 0, 1), near, moved(near, 0, 1))

    own_sources = gathered(own_pack)
    low_sources = gathered(moved(up_pack, 1, 0))
    up_sources = gathered(moved(down_pack, -1, 0))

    lower, upper = jnp.maximum(part - 1, 0), jnp.minimum(part + 1, parts - 1)
    is_first = (part == 0).astype(jnp.int32)
    is_last = (part == parts - 1).astype(jnp.int32)
    place = jnp.stack([col.astype(jnp.int32), is_first, is_last])
    slot = jnp.arange(KA, dtype=jnp.int32)[None, :]
    cols = jnp.where(slot < 5, a_cols - part * NB, a_cols).reshape(NB * KA)

    def aggs_at(which):
        rows = lax.dynamic_slice_in_dim(p_aggs, which * NB, NB, 0) - which * NAG
        return rows

    own_aggs = aggs_at(part)
    low_aggs = aggs_at(lower).reshape(NB * KP)
    up_aggs = aggs_at(upper).reshape(NB * KP)
    low_list = lax.dynamic_slice(halo_rows, (lower, 1, 0), (1, 1, NS)).reshape(NS)
    up_list = lax.dynamic_slice(halo_rows, (upper, 0, 0), (1, 1, NS)).reshape(NS)

    order = jnp.stack([jnp.bitwise_xor(col, f) + NAG * e for f in (3, 1, 2, 0) for e in (0, 1)])
    live = jnp.arange(NB, dtype=jnp.int32) < live_rows[0]
    mask = (own_aggs.T[None, :, :] == order[:, None, None]) & live[None, None, :]
    mask = jnp.repeat(mask.reshape(8 * KP, NB).astype(F32), W, axis=1)
    spread = pl.pallas_call(
        spread_kernel,
        out_shape=jax.ShapeDtypeStruct((8 * BC, ROWS), BF16),
        in_specs=[whole_vmem(), whole_vmem()],
        out_specs=whole_vmem(),
        compiler_params=params(),
        cost_estimate=pl.CostEstimate(flops=10**9, bytes_accessed=4 * 10**6, transcendentals=0),
    )(p_flat, mask)

    a_low = lax.slice_in_dim(a_flat, 480, 736, axis=1)
    a_up = lax.slice_in_dim(a_flat, 608, 864, axis=1)
    own_shape = jax.ShapeDtypeStruct((ROWS, 512), F32)
    own_below, own_above = pl.pallas_call(
        own_kernel,
        out_shape=[own_shape, own_shape],
        in_specs=[smem()] * 3 + [anywhere()] * 4 + [whole_vmem()] * 3,
        out_specs=[whole_vmem(), whole_vmem()],
        scratch_shapes=[
            pltpu.VMEM((4, ROWS + 192, 256), BF16),
            pltpu.VMEM((NB, BW, 1024), BF16),
            pltpu.SemaphoreType.DMA((4,)),
        ],
        compiler_params=params(),
        cost_estimate=pl.CostEstimate(flops=4 * 10**9, bytes_accessed=14 * 10**6, transcendentals=0),
    )(place, cols, own_aggs.reshape(NB * KP), *own_sources, a_flat, a_low, a_up)

    def halo_terms(upper_side, rows_list, aggs, sources, a_part, own):
        return pl.pallas_call(
            make_halo_kernel(upper_side),
            out_shape=[
                jax.ShapeDtypeStruct((4 * BC, 8 * BC), BF16),
                jax.ShapeDtypeStruct((4 * BC, 8 * BC), F32),
            ],
            in_specs=[smem()] * 4 + [anywhere()] * 4 + [whole_vmem()] * 3,
            out_specs=[whole_vmem(), whole_vmem()],
            scratch_shapes=[
                pltpu.VMEM((4, NS * W + 96, 256), BF16),
                pltpu.VMEM((NS, BW, 1024), BF16),
                pltpu.VMEM((ROWS, 1024), BF16),
                pltpu.SemaphoreType.DMA((4,)),
            ],
            compiler_params=params(),
            cost_estimate=pl.CostEstimate(
                flops=5 * 10**9, bytes_accessed=14 * 10**6, transcendentals=0
            ),
        )(place, cols, rows_list, aggs, *sources, a_part, own, spread)

    def summed(send, keep):
        came = moved(send, 0, 1)
        both = keep + came.astype(F32)
        far = moved(both[: 2 * BC].astype(BF16), 0, 2)
        mine = both[2 * BC :] + far.astype(F32)
        return mine[:BC], moved(mine[BC:].astype(BF16), 1, 0)

    low_own, low_next = summed(*halo_terms(False, low_list, low_aggs, low_sources, a_low, own_below))
    up_own, up_next = summed(*halo_terms(True, up_list, up_aggs, up_sources, a_up, own_above))
    band = NAG * BC
    own = jnp.concatenate([low_own, up_own], axis=1)
    came = jnp.concatenate([low_next, up_next], axis=1).astype(F32)
    result = jnp.pad(own, ((0, 0), (band, 0))) + jnp.pad(came, ((0, 0), (0, band)))
    return result.astype(BF16)


def solution(mesh):
    in_specs = (P("dom", "col", None), P("dom", "col", None), P("dom", None), P(), P(), P("dom"))
    out_specs = P(("dom", "col"), None)
    return jax.shard_map(local, mesh=mesh, in_specs=in_specs, out_specs=out_specs, check_vma=False)
```

```python
import jax
import jax.numpy as jnp
from jax import lax
from jax.experimental import pallas as pl
from jax.experimental.pallas import tpu as pltpu
from jax.sharding import PartitionSpec as P

BW = 96
BC = 96
KA = 9
KP = 3
NAG = 4
NB = 64
NS = 32
W = 24
ROWS = NB * W
PACK = NS * W + 96
UN = 4
STEPS = NB // UN
AXES = ("dom", "col")
VMEM_LIMIT = 56 * 1024 * 1024
F32, BF16, I32 = jnp.float32, jnp.bfloat16, jnp.int32


def params():
    return pltpu.CompilerParams(vmem_limit_bytes=VMEM_LIMIT)


def cost(microseconds):
    flops = int(microseconds * 1.1e9)
    return pl.CostEstimate(flops=flops, bytes_accessed=10**6, transcendentals=0)


def in_vmem():
    return pl.BlockSpec(memory_space=pltpu.VMEM)


def in_smem():
    return pl.BlockSpec(memory_space=pltpu.SMEM)


def anywhere():
    return pl.BlockSpec(memory_space=pl.ANY)


def window_start(part, parts):
    return jnp.clip((part - 1) * NB, 0, (parts - 3) * NB)


def fill_order(part, halo_ref, order_ref, inverse):
    def step(r, taken):
        here = halo_ref[part, 0, jnp.minimum(taken, NS - 1)]
        is_listed = jnp.logical_and(taken < NS, here == r).astype(I32)
        at = jnp.where(is_listed == 1, taken, NS + r - taken)
        if inverse:
            order_ref[r] = at
        else:
            order_ref[at] = r
        return taken + is_listed

    lax.fori_loop(0, NB, step, jnp.int32(0))


def pack_kernel(place_ref, halo_ref, p_ref, listed_ref, others_ref, up_ref, wide_ref, order_ref):
    part = place_ref[0]
    fill_order(part, halo_ref, order_ref, False)

    def widen(t, carry):
        pair = p_ref[pl.ds(pl.multiple_of(t * 48, 48), 48), :].astype(F32)
        wide_ref[2 * t] = pair[0:24]
        wide_ref[2 * t + 1] = pair[24:48]
        return carry

    lax.fori_loop(0, NB // 2, widen, 0, unroll=4)
    picks = (
        (listed_ref, lambda n: order_ref[n]),
        (others_ref, lambda n: order_ref[NS + n]),
        (up_ref, lambda n: halo_ref[part, 1, n]),
    )
    for out_ref, row_of in picks:
        for g in range(NS // 16):
            tails = []
            for q in range(8):
                t = 8 * g + q
                two = [wide_ref[row_of(2 * t)], wide_ref[row_of(2 * t + 1)]]
                pair = jnp.concatenate(two, axis=0).astype(BF16)
                out_ref[48 * t : 48 * t + 48, :] = pair[:, 0:256]
                tails.append(pair[:, 256:288])
            start = NS * W + 48 * g
            out_ref[start : start + 48, :] = jnp.concatenate(tails, axis=1)


def split96(tiles, lane):
    x0, x1, x2 = tiles
    second = jnp.where(lane < 32, pltpu.roll(x0, 32, 1), pltpu.roll(x1, 32, 1))
    third = jnp.where(lane < 64, pltpu.roll(x1, 64, 1), pltpu.roll(x2, 64, 1))
    return x0, second, third, pltpu.roll(x2, 96, 1)


def prepare_kernel(place_ref, aggs_ref, live_ref, p_ref, a_ref, spread_ref, blocks_ref, wide_ref, *, parts):
    part, col = place_ref[0], place_ref[1]
    own = part * NB - window_start(part, parts)
    lane = lax.broadcasted_iota(I32, (48, 128), 1)
    wide_ref[...] = jnp.zeros_like(wide_ref)

    def pair(t, carry):
        rows = pl.ds(pl.multiple_of(t * 48, 48), 48)
        for g in range(2):
            tiles = [a_ref[rows, 384 * g + 128 * x : 384 * g + 128 * x + 128].astype(F32) for x in range(3)]
            for k, block in enumerate(split96(tiles, lane)):
                blocks_ref[4 * g + k, rows, :] = block.astype(BF16)
        blocks_ref[8, rows, 0:96] = a_ref[rows, 768:864]
        p = p_ref[rows, :].astype(F32)
        x0, x1 = p[:, 0:128], p[:, 128:256]
        tail = jnp.concatenate([p[:, 256:288], jnp.zeros((48, 96), F32)], axis=1)
        blocks = split96((x0, x1, tail), lane)[:3]
        for odd in range(2):
            r = 2 * t + odd
            live = (r < live_ref[0]).astype(F32)
            for m in range(KP):
                block = aggs_ref[own + r, m] - part * NAG
                after = block // NAG
                turn = jnp.bitwise_xor(block - NAG * after, col)
                at = 2 * (3 - (2 * (turn % 2) + turn // 2)) + after
                value = jnp.where(lane < 96, blocks[m], 0.0)[24 * odd : 24 * odd + 24] * live
                wide_ref[at, pl.ds(pl.multiple_of(r * W, 8), W), :] = value
        return carry

    lax.fori_loop(0, NB // 2, pair, 0, unroll=2)
    eye = (
        lax.broadcasted_iota(I32, (BC, 128), 0) == lax.broadcasted_iota(I32, (BC, 128), 1)
    ).astype(F32).astype(BF16)
    for b in range(8):
        for n in range(3):
            flipped = lax.dot_general(
                eye,
                wide_ref[b, 512 * n : 512 * n + 512, :].astype(BF16),
                (((1,), (1,)), ((), ())),
                preferred_element_type=F32,
            )
            spread_ref[BC * b : BC * b + BC, 512 * n : 512 * n + 512] = flipped.astype(BF16)


def unpack(sources, prolong, first):
    lane = lax.broadcasted_iota(I32, (48, 128), 1)

    def group(g, carry):
        tails = []
        for v in range(4):
            rows = pl.ds(pl.multiple_of(NS * W + g * 48, 48), 48)
            tails.append([sources[v, rows, 128 * h : 128 * h + 128].astype(F32) for h in range(2)])
        for q in range(8):
            t = 8 * g + q
            parts = [[], [], []]
            for v in range(4):
                rows = pl.ds(pl.multiple_of(t * 48, 48), 48)
                x0 = sources[v, rows, 0:128].astype(F32)
                x1 = sources[v, rows, 128:256].astype(F32)
                tail, shift = tails[v][q // 4], (64 - 32 * (q % 4)) % 128
                if shift:
                    tail = pltpu.roll(tail, shift, 1)
                parts[0].append(x0)
                parts[1].append(jnp.where(lane < 32, pltpu.roll(x0, 32, 1), pltpu.roll(x1, 32, 1)))
                parts[2].append(jnp.where(lane < 64, pltpu.roll(x1, 64, 1), tail))
            for j in range(KP):
                for odd in range(2):
                    rows = [x[24 * odd : 24 * odd + 24] for x in parts[j]]
                    block = jnp.concatenate(rows, axis=0).astype(BF16)
                    prolong[first + 2 * t + odd, :, 128 * j : 128 * j + 128] = block
        return carry

    lax.fori_loop(0, NS // 16, group, 0)


def fetches(refs, scratch, sems, col):
    return [
        pltpu.make_async_copy(ref, scratch.at[jnp.bitwise_xor(col, s)], sems.at[s])
        for s, ref in enumerate(refs)
    ]


def add_products(step, slots, a_ref, first_slot, prolong, row_of, blocks_of, sums):
    for slot in slots:
        for u in range(UN):
            i = UN * step + u
            odd = u % 2
            start = pl.multiple_of(step * (UN * W) + 48 * (u // 2) + 16 * odd, 16)
            at = row_of(i, slot)
            got = jnp.dot(
                a_ref[slot - first_slot, pl.ds(start, 32), 0:BW], prolong[at[0]], preferred_element_type=F32
            )[8 * odd : 8 * odd + 24]
            where = blocks_of(at[1])
            held = [sums[u][step, c] for c in where]
            for j in range(KP):
                sums[u][step, where[j]] = held[j] + got[:, 128 * j : 128 * j + 128]


def own_kernel(place_ref, halo_ref, aggs_ref, cols_ref, *refs, parts):
    listed, others, a_hbm, out_hbm = refs[0:4], refs[4:8], refs[8], refs[9]
    sources, prolong, a_ref, s0, s1, s2, s3, order_ref, in_sems, a_sem, out_sems = refs[10:]
    sums = (s0, s1, s2, s3)
    part, col = place_ref[0], place_ref[1]
    own = part * NB - window_start(part, parts)
    base = part * NAG
    copies = [
        fetches(listed, sources.at[0], in_sems.at[0], col),
        fetches(others, sources.at[1], in_sems.at[1], col),
    ]
    a_copy = pltpu.make_async_copy(a_hbm, a_ref, a_sem)
    for copy in copies[0] + copies[1]:
        copy.start()
    a_copy.start()
    fill_order(part, halo_ref, order_ref, True)
    for each in sums:
        each[...] = jnp.zeros_like(each)
    for half in range(2):
        for copy in copies[half]:
            copy.wait()
        unpack(sources.at[half], prolong, NS * half)
    a_copy.wait()

    def row_of(i, slot):
        row = cols_ref[i, slot]
        if slot < 5:
            row = row - part * NB
        return order_ref[row], row

    def blocks_of(row):
        return [aggs_ref[own + row, j] - base for j in range(KP)]

    def run(slots, first, count):
        def step(n, carry):
            add_products(first + n, slots, a_ref, 0, prolong, row_of, blocks_of, sums)
            return carry

        lax.fori_loop(0, count, step, 0)

    @pl.when(part == 0)
    def _():
        run((5, 6), 0, STEPS)

    @pl.when(part == parts - 1)
    def _():
        run((7, 8), 0, STEPS)

    leaving = []
    for chunk in range(4):
        run((0, 1, 2, 3, 4), 4 * chunk, 4)
        for u in range(UN):
            copy = pltpu.make_async_copy(
                sums[u].at[4 * chunk : 4 * chunk + 4],
                out_hbm.at[u, 4 * chunk : 4 * chunk + 4],
                out_sems.at[chunk, u],
            )
            copy.start()
            leaving.append(copy)
    for copy in leaving:
        copy.wait()


def halo_kernel(place_ref, halo_ref, aggs_ref, cols_ref, *refs, parts, upper):
    packed, a_hbm, own_hbm, spread_hbm, send_ref, keep_ref = refs[0:4], *refs[4:9]
    sources, prolong, a_ref, s0, s1, s2, s3, spread, coupled, in_sems, own_sems, sems = refs[9:]
    sums = (s0, s1, s2, s3)
    part, col = place_ref[0], place_ref[1]
    first_slot = 7 if upper else 5
    other = jnp.minimum(part + 1, parts - 1) if upper else jnp.maximum(part - 1, 0)
    rows_at = other * NB - window_start(part, parts)
    own_at, new_at = (0, NAG) if upper else (NAG, 0)
    copies = fetches(packed, sources, in_sems, col)
    a_copy = pltpu.make_async_copy(a_hbm.at[first_slot : first_slot + 2], a_ref, sems.at[0])
    spread_copy = pltpu.make_async_copy(spread_hbm, spread, sems.at[1])
    own_copies = [
        pltpu.make_async_copy(
            own_hbm.at[u, :, (NAG if upper else 0) : (NAG if upper else 0) + NAG],
            sums[u].at[:, own_at : own_at + NAG],
            own_sems.at[u],
        )
        for u in range(UN)
    ]
    for copy in copies + [a_copy] + own_copies + [spread_copy]:
        copy.start()
    for each in sums:
        each[:, new_at : new_at + NAG] = jnp.zeros((STEPS, NAG, W, 128), F32)
    for copy in copies:
        copy.wait()
    unpack(sources, prolong, 0)
    for copy in [a_copy] + own_copies:
        copy.wait()
    lane = lax.broadcasted_iota(I32, (48, 128), 1)

    def row_of(i, slot):
        at = cols_ref[i, slot]
        return at, rows_at + halo_ref[other, 0 if upper else 1, at]

    def blocks_of(row):
        return [aggs_ref[row, j] - other * NAG for j in range(KP)]

    def step(n, carry):
        add_products(n, (first_slot, first_slot + 1), a_ref, first_slot, prolong, row_of, blocks_of, sums)
        for two in range(2):
            rows = pl.ds(pl.multiple_of(n * (UN * W) + 48 * two, 48), 48)
            for half in range(2):
                y0, y1, y2, y3 = [
                    jnp.concatenate([sums[2 * two][n, c], sums[2 * two + 1][n, c]], axis=0)
                    for c in range(4 * half, 4 * half + 4)
                ]
                y1, y2, y3 = pltpu.roll(y1, 96, 1), pltpu.roll(y2, 64, 1), pltpu.roll(y3, 32, 1)
                tiles = [
                    jnp.where(lane < 96, y0, y1),
                    jnp.where(lane < 64, y1, y2),
                    jnp.where(lane < 32, y2, y3),
                ]
                for x in range(3):
                    at = 384 * half + 128 * x
                    coupled[rows, at : at + 128] = tiles[x].astype(BF16)
        return carry

    lax.fori_loop(0, STEPS, step, 0)
    spread_copy.wait()
    for n in range(3):
        at = slice(256 * n, 256 * n + 256)
        for half, out_ref in ((0, send_ref), (1, keep_ref)):
            got = jnp.dot(
                spread[384 * half : 384 * half + 384, :], coupled[:, at], preferred_element_type=F32
            )
            out_ref[:, at] = got.astype(out_ref.dtype)


def local(a_vals, p_vals, a_cols, p_aggs, halo_rows, live_rows):
    part = lax.axis_index("dom")
    parts = lax.axis_size("dom")
    col = lax.axis_index("col")
    cols_count = lax.axis_size("col")
    devices = [(d, c) for d in range(parts) for c in range(cols_count)]

    def moved(x, step, flip):
        route = [
            (d * cols_count + c, (d + step) * cols_count + (c ^ flip))
            for d, c in devices
            if 0 <= d + step < parts
        ]
        return lax.ppermute(x, AXES, route)

    place = jnp.stack([part, col]).astype(I32)
    p_flat = p_vals.reshape(ROWS, KP * BC)
    a_flat = a_vals.reshape(ROWS, KA * BW)
    packed = jax.ShapeDtypeStruct((PACK, 256), BF16)
    listed, others, upward = pl.pallas_call(
        pack_kernel,
        out_shape=[packed] * 3,
        in_specs=[in_smem(), in_smem(), in_vmem()],
        out_specs=[in_vmem()] * 3,
        scratch_shapes=[pltpu.VMEM((NB, W, KP * BC), F32), pltpu.SMEM((NB,), I32)],
        compiler_params=params(),
        cost_estimate=cost(4),
    )(place, halo_rows, p_flat)

    near_listed = moved(listed, 0, 2)
    near_others = moved(others, 0, 2)
    low = moved(upward, 1, 0)
    up = moved(listed, -1, 0)
    up_far = moved(near_listed, -1, 0)
    low_far = moved(low, 0, 2)

    def both_cores(x, far):
        return (x, moved(x, 0, 1), far, moved(far, 0, 1))

    aggs = lax.dynamic_slice_in_dim(p_aggs, window_start(part, parts), 3 * NB, 0)
    spread, blocks = pl.pallas_call(
        lambda *refs: prepare_kernel(*refs, parts=parts),
        out_shape=[
            jax.ShapeDtypeStruct((8 * BC, ROWS), BF16),
            jax.ShapeDtypeStruct((KA, ROWS, 128), BF16),
        ],
        in_specs=[in_smem()] * 3 + [in_vmem()] * 2,
        out_specs=[in_vmem(), in_vmem()],
        scratch_shapes=[pltpu.VMEM((8, ROWS, 128), F32)],
        compiler_params=params(),
        cost_estimate=cost(9),
    )(place, aggs, live_rows, p_flat, a_flat)

    sums_scratch = [pltpu.VMEM((STEPS, 8, W, 128), F32)] * UN
    own = pl.pallas_call(
        lambda *refs: own_kernel(*refs, parts=parts),
        out_shape=jax.ShapeDtypeStruct((UN, STEPS, 8, W, 128), F32),
        in_specs=[in_smem()] * 4 + [anywhere()] * 9,
        out_specs=anywhere(),
        scratch_shapes=[
            pltpu.VMEM((2, 4, PACK, 256), BF16),
            pltpu.VMEM((NB, BW, KP * 128), BF16),
            pltpu.VMEM((KA, ROWS, 128), BF16),
            *sums_scratch,
            pltpu.SMEM((NB,), I32),
            pltpu.SemaphoreType.DMA((2, 4)),
            pltpu.SemaphoreType.DMA,
            pltpu.SemaphoreType.DMA((4, UN)),
        ],
        compiler_params=params(),
        cost_estimate=cost(10),
    )(place, halo_rows, aggs, a_cols, *both_cores(listed, near_listed), *both_cores(others, near_others), blocks)

    def halo_terms(upper, sources):
        return pl.pallas_call(
            lambda *refs: halo_kernel(*refs, parts=parts, upper=upper),
            out_shape=[
                jax.ShapeDtypeStruct((4 * BC, 8 * BC), BF16),
                jax.ShapeDtypeStruct((4 * BC, 8 * BC), F32),
            ],
            in_specs=[in_smem()] * 4 + [anywhere()] * 7,
            out_specs=[in_vmem(), in_vmem()],
            scratch_shapes=[
                pltpu.VMEM((4, PACK, 256), BF16),
                pltpu.VMEM((NS, BW, KP * 128), BF16),
                pltpu.VMEM((2, ROWS, 128), BF16),
                *sums_scratch,
                pltpu.VMEM((8 * BC, ROWS), BF16),
                pltpu.VMEM((ROWS, 8 * BC), BF16),
                pltpu.SemaphoreType.DMA((4,)),
                pltpu.SemaphoreType.DMA((UN,)),
                pltpu.SemaphoreType.DMA((2,)),
            ],
            compiler_params=params(),
            cost_estimate=cost(8),
        )(place, halo_rows, aggs, a_cols, *sources, blocks, own, spread)

    def summed(send, keep):
        both = keep + moved(send, 0, 1).astype(F32)
        away = both.astype(BF16)
        far_own = moved(away[0:BC], 0, 2)
        far_next = moved(away[BC : 2 * BC], 1, 2)
        near_next = moved(away[3 * BC :], 1, 0)
        mine = both[2 * BC : 3 * BC] + far_own.astype(F32)
        return mine, far_next.astype(F32) + near_next.astype(F32)

    low_own, low_next = summed(*halo_terms(False, both_cores(low, low_far)))
    up_own, up_next = summed(*halo_terms(True, both_cores(up, up_far)))
    band = NAG * BC
    mine = jnp.concatenate([low_own, up_own], axis=1)
    came = jnp.concatenate([low_next, up_next], axis=1)
    result = jnp.pad(mine, ((0, 0), (band, 0))) + jnp.pad(came, ((0, 0), (0, band)))
    return result.astype(BF16)


def solution(mesh):
    in_specs = (P("dom", "col", None), P("dom", "col", None), P("dom", None), P(), P(), P("dom"))
    out_specs = P(("dom", "col"), None)
    return jax.shard_map(local, mesh=mesh, in_specs=in_specs, out_specs=out_specs, check_vma=False)
```

```python
import jax
import jax.numpy as jnp
from jax import lax
from jax.experimental import pallas as pl
from jax.experimental.pallas import tpu as pltpu
from jax.sharding import PartitionSpec as P

BW = 96
BC = 96
KA = 9
KP = 3
NAG = 4
NB = 64
NS = 32
W = 24
ROWS = NB * W
UN = 4
STEPS = NB // UN
AXES = ("dom", "col")
VMEM_LIMIT = 16 * 1024 * 1024
F32, BF16, I32 = jnp.float32, jnp.bfloat16, jnp.int32


def params():
    return pltpu.CompilerParams(vmem_limit_bytes=VMEM_LIMIT)


def cost(microseconds):
    flops = int(microseconds * 1.1e9)
    return pl.CostEstimate(flops=flops, bytes_accessed=10**6, transcendentals=0)


def in_vmem():
    return pl.BlockSpec(memory_space=pltpu.VMEM)


def in_smem():
    return pl.BlockSpec(memory_space=pltpu.SMEM)


def window_start(part, parts):
    return jnp.clip((part - 1) * NB, 0, (parts - 3) * NB)


def packed(count):
    return jax.ShapeDtypeStruct((count * W + count * W // 8, 256), BF16)


def pack_own_kernel(p_ref, out_ref):
    out_ref[0:ROWS, :] = p_ref[:, 0:256]
    for g in range(NB // 16):
        tails = [p_ref[48 * (8 * g + q) : 48 * (8 * g + q) + 48, 256:288] for q in range(8)]
        out_ref[ROWS + 48 * g : ROWS + 48 * g + 48, :] = jnp.concatenate(tails, axis=1)


def pack_rows(wide_ref, row_of, out_ref):
    for g in range(NS // 16):
        tails = []
        for q in range(8):
            t = 8 * g + q
            two = [wide_ref[row_of(2 * t + odd)] for odd in range(2)]
            pair = jnp.concatenate(two, axis=0).astype(BF16)
            out_ref[48 * t : 48 * t + 48, :] = pair[:, 0:256]
            tails.append(pair[:, 256:288])
        start = NS * W + 48 * g
        out_ref[start : start + 48, :] = jnp.concatenate(tails, axis=1)


def pack_halo_kernel(place_ref, halo_ref, p_ref, down_ref, up_ref, wide_ref):
    part = place_ref[0]

    def widen(t, carry):
        pair = p_ref[pl.ds(pl.multiple_of(t * 48, 48), 48), :].astype(F32)
        wide_ref[2 * t] = pair[0:24]
        wide_ref[2 * t + 1] = pair[24:48]
        return carry

    lax.fori_loop(0, NB // 2, widen, 0, unroll=4)
    pack_rows(wide_ref, lambda n: halo_ref[part, 1, n], up_ref)
    pack_rows(wide_ref, lambda n: halo_ref[part, 0, n], down_ref)


def select_kernel(place_ref, halo_ref, packed_ref, down_ref, wide_ref):
    part = place_ref[0]

    def widen(g, carry):
        tail = packed_ref[pl.ds(pl.multiple_of(ROWS + g * 48, 48), 48), :].astype(F32)
        for q in range(8):
            t = 8 * g + q
            pair = packed_ref[pl.ds(pl.multiple_of(t * 48, 48), 48), :].astype(F32)
            for odd in range(2):
                rows = slice(24 * odd, 24 * odd + 24)
                wide_ref[2 * t + odd, :, 0:256] = pair[rows]
                wide_ref[2 * t + odd, :, 256:288] = tail[rows, 32 * q : 32 * q + 32]
        return carry

    lax.fori_loop(0, NB // 16, widen, 0)
    pack_rows(wide_ref, lambda n: halo_ref[part, 0, n], down_ref)


def prepare_kernel(place_ref, aggs_ref, live_ref, p_ref, a_ref, spread_ref, blocks_ref, wide_ref, *, parts):
    part, col = place_ref[0], place_ref[1]
    own = part * NB - window_start(part, parts)
    lane = lax.broadcasted_iota(I32, (48, 128), 1)
    wide_ref[...] = jnp.zeros_like(wide_ref)
    to = lax.broadcasted_iota(I32, (256, 128), 1)
    come = W * jnp.bitwise_xor(to // W, col) + to % W
    at = lax.broadcasted_iota(I32, (256, 128), 0)

    def one_hot(shift):
        return jnp.logical_and(at == come + shift, to < BW).astype(F32).astype(BF16)

    for k in range(KA):
        start = BW * k // 128 * 128
        stop = min(start + 256, KA * BW)
        pick = one_hot(BW * k - start)[0 : stop - start]
        for n in range(3):
            rows = slice(512 * n, 512 * n + 512)
            got = jnp.dot(a_ref[rows, start:stop], pick, preferred_element_type=F32)
            blocks_ref[k, rows, :] = got.astype(BF16)

    def pair(t, carry):
        rows = pl.ds(pl.multiple_of(t * 48, 48), 48)
        p = p_ref[rows, :].astype(F32)
        x0, x1 = p[:, 0:128], p[:, 128:256]
        tail = jnp.concatenate([p[:, 256:288], jnp.zeros((48, 96), F32)], axis=1)
        blocks = (
            x0,
            jnp.where(lane < 32, pltpu.roll(x0, 32, 1), pltpu.roll(x1, 32, 1)),
            jnp.where(lane < 64, pltpu.roll(x1, 64, 1), pltpu.roll(tail, 64, 1)),
        )
        for odd in range(2):
            r = 2 * t + odd
            live = (r < live_ref[0]).astype(F32)
            for m in range(KP):
                block = aggs_ref[KP * (own + r) + m] - part * NAG
                after = block // NAG
                turn = jnp.bitwise_xor(block - NAG * after, col)
                place = 2 * (3 - (2 * (turn % 2) + turn // 2)) + after
                value = jnp.where(lane < 96, blocks[m], 0.0)[24 * odd : 24 * odd + 24] * live
                wide_ref[place, pl.ds(pl.multiple_of(r * W, 8), W), :] = value
        return carry

    lax.fori_loop(0, NB // 2, pair, 0, unroll=2)
    eye = (
        lax.broadcasted_iota(I32, (BC, 128), 0) == lax.broadcasted_iota(I32, (BC, 128), 1)
    ).astype(F32).astype(BF16)
    for b in range(8):
        for n in range(3):
            flipped = lax.dot_general(
                eye,
                wide_ref[b, 512 * n : 512 * n + 512, :].astype(BF16),
                (((1,), (1,)), ((), ())),
                preferred_element_type=F32,
            )
            spread_ref[BC * b : BC * b + BC, 512 * n : 512 * n + 512] = flipped.astype(BF16)


def unpack(count, sources, prolong):
    lane = lax.broadcasted_iota(I32, (48, 128), 1)

    def group(g, carry):
        tails = []
        for source in sources:
            rows = pl.ds(pl.multiple_of(count * W + g * 48, 48), 48)
            tails.append([source[rows, 128 * h : 128 * h + 128].astype(F32) for h in range(2)])
        for q in range(8):
            t = 8 * g + q
            parts = [[], [], []]
            for v, source in enumerate(sources):
                rows = pl.ds(pl.multiple_of(t * 48, 48), 48)
                x0 = source[rows, 0:128].astype(F32)
                x1 = source[rows, 128:256].astype(F32)
                tail, shift = tails[v][q // 4], (64 - 32 * (q % 4)) % 128
                if shift:
                    tail = pltpu.roll(tail, shift, 1)
                parts[0].append(x0)
                parts[1].append(jnp.where(lane < 32, pltpu.roll(x0, 32, 1), pltpu.roll(x1, 32, 1)))
                parts[2].append(jnp.where(lane < 64, pltpu.roll(x1, 64, 1), tail))
            for j in range(KP):
                for odd in range(2):
                    rows = [x[24 * odd : 24 * odd + 24] for x in parts[j]]
                    block = jnp.concatenate(rows, axis=0).astype(BF16)
                    prolong[2 * t + odd, :, 128 * j : 128 * j + 128] = block
        return carry

    lax.fori_loop(0, count // 16, group, 0)


def add_products(step, slots, a_ref, prolong, row_of, blocks_of, sums):
    for slot in slots:
        for u in range(UN):
            i = UN * step + u
            odd = u % 2
            start = pl.multiple_of(step * (UN * W) + 48 * (u // 2) + 16 * odd, 16)
            at = row_of(i, slot)
            got = jnp.dot(
                a_ref[slot, pl.ds(start, 32), 0:BW], prolong[at[0]], preferred_element_type=F32
            )[8 * odd : 8 * odd + 24]
            where = blocks_of(at[1])
            held = [sums[u][step, c] for c in where]
            for j in range(KP):
                sums[u][step, where[j]] = held[j] + got[:, 128 * j : 128 * j + 128]


def own_kernel(place_ref, aggs_ref, cols_ref, *refs, parts):
    sources, a_ref, sums, prolong = refs[0:4], refs[4], refs[5:9], refs[9]
    part = place_ref[0]
    own = part * NB - window_start(part, parts)
    base = part * NAG
    unpack(NB, sources, prolong)

    def row_of(i, slot):
        row = cols_ref[KA * i + slot]
        if slot < 5:
            row = row - part * NB
        return row, row

    def blocks_of(row):
        return [aggs_ref[KP * (own + row) + j] - base for j in range(KP)]

    def run(slots, fresh):
        def step(n, carry):
            if fresh:
                for each in sums:
                    each[n] = jnp.zeros((8, W, 128), F32)
            add_products(n, slots, a_ref, prolong, row_of, blocks_of, sums)
            return carry

        lax.fori_loop(0, STEPS, step, 0, unroll=2 if fresh else 1)

    run((0, 1, 2, 3, 4), True)

    @pl.when(part == 0)
    def _():
        run((5, 6), False)

    @pl.when(part == parts - 1)
    def _():
        run((7, 8), False)


def halo_kernel(place_ref, halo_ref, aggs_ref, cols_ref, *refs, parts, upper):
    sources, a_ref, own, spread, send_ref, keep_ref = refs[0:4], refs[4], refs[5:9], *refs[9:12]
    prolong, sums, coupled = refs[12], refs[13:17], refs[17]
    part = place_ref[0]
    slots = (7, 8) if upper else (5, 6)
    other = jnp.minimum(part + 1, parts - 1) if upper else jnp.maximum(part - 1, 0)
    rows_at = other * NB - window_start(part, parts)
    inside = part < parts - 1 if upper else part > 0

    @pl.when(inside)
    def _():
        unpack(NS, sources, prolong)

    lane = lax.broadcasted_iota(I32, (48, 128), 1)

    def row_of(i, slot):
        at = cols_ref[KA * i + slot]
        return at, rows_at + halo_ref[other, 0 if upper else 1, at]

    def blocks_of(row):
        return [aggs_ref[KP * row + j] - other * NAG for j in range(KP)]

    def sum_of(n, u, c):
        if upper:
            return sums[u][n, c] + own[u][n, NAG + c] if c < NAG else sums[u][n, c]
        return sums[u][n, c] + own[u][n, c - NAG] if c >= NAG else sums[u][n, c]

    def run(products):
        def step(n, carry):
            for each in sums:
                each[n] = jnp.zeros((8, W, 128), F32)
            if products:
                add_products(n, slots, a_ref, prolong, row_of, blocks_of, sums)
            for two in range(2):
                rows = pl.ds(pl.multiple_of(n * (UN * W) + 48 * two, 48), 48)
                for half in range(2):
                    y0, y1, y2, y3 = [
                        jnp.concatenate([sum_of(n, 2 * two, c), sum_of(n, 2 * two + 1, c)], axis=0)
                        for c in range(4 * half, 4 * half + 4)
                    ]
                    y1, y2, y3 = pltpu.roll(y1, 96, 1), pltpu.roll(y2, 64, 1), pltpu.roll(y3, 32, 1)
                    tiles = [
                        jnp.where(lane < 96, y0, y1),
                        jnp.where(lane < 64, y1, y2),
                        jnp.where(lane < 32, y2, y3),
                    ]
                    for x in range(3):
                        at = 384 * half + 128 * x
                        coupled[rows, at : at + 128] = tiles[x].astype(BF16)
            return carry

        lax.fori_loop(0, STEPS, step, 0, unroll=2 if products else 1)

    @pl.when(inside)
    def _():
        run(True)

    @pl.when(jnp.logical_not(inside))
    def _():
        run(False)

    for n in range(3):
        at = slice(256 * n, 256 * n + 256)
        for half, out_ref in ((0, send_ref), (1, keep_ref)):
            got = jnp.dot(
                spread[384 * half : 384 * half + 384, :], coupled[:, at], preferred_element_type=F32
            )
            out_ref[:, at] = got.astype(out_ref.dtype)


def local(a_vals, p_vals, a_cols, p_aggs, halo_rows, live_rows):
    part = lax.axis_index("dom")
    parts = lax.axis_size("dom")
    col = lax.axis_index("col")
    cols_count = lax.axis_size("col")
    devices = [(d, c) for d in range(parts) for c in range(cols_count)]

    def moved(x, step, flip):
        route = [
            (d * cols_count + c, (d + step) * cols_count + (c ^ flip))
            for d, c in devices
            if 0 <= d + step < parts
        ]
        return lax.ppermute(x, AXES, route)

    place = jnp.stack([part, col]).astype(I32)
    p_flat = p_vals.reshape(ROWS, KP * BC)
    a_flat = a_vals.reshape(ROWS, KA * BW)
    own_pack = pl.pallas_call(
        pack_own_kernel,
        out_shape=packed(NB),
        in_specs=[in_vmem()],
        out_specs=in_vmem(),
        compiler_params=params(),
        cost_estimate=cost(2),
    )(p_flat)
    near = moved(own_pack, 0, 2)
    down, upward = pl.pallas_call(
        pack_halo_kernel,
        out_shape=[packed(NS)] * 2,
        in_specs=[in_smem(), in_smem(), in_vmem()],
        out_specs=[in_vmem()] * 2,
        scratch_shapes=[pltpu.VMEM((NB, W, KP * BC), F32)],
        compiler_params=params(),
        cost_estimate=cost(3),
    )(place, halo_rows, p_flat)
    low = moved(upward, 1, 0)
    up = moved(down, -1, 0)

    def both_cores(x, far):
        return (x, moved(x, 0, 1), far, moved(far, 0, 1))

    aggs = lax.dynamic_slice_in_dim(p_aggs, window_start(part, parts), 3 * NB, 0).reshape(3 * NB * KP)
    cols = a_cols.reshape(NB * KA)
    spread, blocks = pl.pallas_call(
        lambda *refs: prepare_kernel(*refs, parts=parts),
        out_shape=[
            jax.ShapeDtypeStruct((8 * BC, ROWS), BF16),
            jax.ShapeDtypeStruct((KA, ROWS, 128), BF16),
        ],
        in_specs=[in_smem()] * 3 + [in_vmem()] * 2,
        out_specs=[in_vmem()] * 2,
        scratch_shapes=[pltpu.VMEM((8, ROWS, 128), F32)],
        compiler_params=params(),
        cost_estimate=cost(9),
    )(place, aggs, live_rows, p_flat, a_flat)
    near, low, spread, blocks = lax.optimization_barrier((near, low, spread, blocks))
    low_far = moved(low, 0, 2)
    up_far = moved(
        pl.pallas_call(
            select_kernel,
            out_shape=packed(NS),
            in_specs=[in_smem(), in_smem(), in_vmem()],
            out_specs=in_vmem(),
            scratch_shapes=[pltpu.VMEM((NB, W, KP * BC), F32)],
            compiler_params=params(),
            cost_estimate=cost(3),
        )(place, halo_rows, near),
        -1,
        0,
    )

    sums_type = jax.ShapeDtypeStruct((STEPS, 8, W, 128), F32)
    own = pl.pallas_call(
        lambda *refs: own_kernel(*refs, parts=parts),
        out_shape=[sums_type] * UN,
        in_specs=[in_smem()] * 3 + [in_vmem()] * 5,
        out_specs=[in_vmem()] * UN,
        scratch_shapes=[pltpu.VMEM((NB, BW, KP * 128), BF16)],
        compiler_params=params(),
        cost_estimate=cost(10),
    )(place, aggs, cols, *both_cores(own_pack, near), blocks)
    up_far, low_far, first_sums = lax.optimization_barrier((up_far, low_far, own[0]))
    own = (first_sums, *own[1:])

    def halo_terms(upper, sources):
        return pl.pallas_call(
            lambda *refs: halo_kernel(*refs, parts=parts, upper=upper),
            out_shape=[
                jax.ShapeDtypeStruct((4 * BC, 8 * BC), BF16),
                jax.ShapeDtypeStruct((4 * BC, 8 * BC), F32),
            ],
            in_specs=[in_smem()] * 4 + [in_vmem()] * (6 + UN),
            out_specs=[in_vmem(), in_vmem()],
            scratch_shapes=[
                pltpu.VMEM((NS, BW, KP * 128), BF16),
                *[pltpu.VMEM((STEPS, 8, W, 128), F32)] * UN,
                pltpu.VMEM((ROWS, 8 * BC), BF16),
            ],
            compiler_params=params(),
            cost_estimate=cost(8),
        )(place, halo_rows, aggs, cols, *sources, blocks, *own, spread)

    low_send, low_keep = halo_terms(False, both_cores(low, low_far))
    low_came = moved(low_send, 0, 1)
    up_send, up_keep = halo_terms(True, both_cores(up, up_far))
    low_came, up_send, up_keep = lax.optimization_barrier((low_came, up_send, up_keep))
    up_came = moved(up_send, 0, 1)
    low_both = low_keep + low_came.astype(F32)
    low_mine = low_both[2 * BC :] + moved(low_both[: 2 * BC].astype(BF16), 0, 2).astype(F32)
    up_both = up_keep + up_came.astype(F32)
    away = up_both.astype(BF16)
    far_own = moved(away[0:BC], 0, 2)
    far_next = moved(away[BC : 2 * BC], 1, 2)
    near_next = moved(jnp.concatenate([low_mine[BC:].astype(BF16), away[3 * BC :]], axis=0), 1, 0)
    low_own, low_next = low_mine[:BC], near_next[:BC].astype(F32)
    up_own = up_both[2 * BC : 3 * BC] + far_own.astype(F32)
    up_next = near_next[BC:].astype(F32) + far_next.astype(F32)
    band = NAG * BC
    mine = jnp.concatenate([low_own, up_own], axis=1)
    came = jnp.concatenate([low_next, up_next], axis=1)
    result = jnp.pad(mine, ((0, 0), (band, 0))) + jnp.pad(came, ((0, 0), (0, band)))
    return result.astype(BF16)


def solution(mesh):
    in_specs = (P("dom", "col", None), P("dom", "col", None), P("dom", None), P(), P(), P("dom"))
    out_specs = P(("dom", "col"), None)
    return jax.shard_map(local, mesh=mesh, in_specs=in_specs, out_specs=out_specs, check_vma=False)
```

```python
import jax
import jax.numpy as jnp
from jax import lax
from jax.experimental import pallas as pl
from jax.experimental.pallas import tpu as pltpu
from jax.sharding import PartitionSpec as P

BW = 96
BC = 96
KA = 9
KP = 3
NAG = 4
NB = 64
NS = 32
W = 24
ROWS = NB * W
UN = 4
STEPS = NB // UN
AXES = ("dom", "col")
VMEM_LIMIT = 16 * 1024 * 1024
F32, BF16, I32 = jnp.float32, jnp.bfloat16, jnp.int32


def params():
    return pltpu.CompilerParams(vmem_limit_bytes=VMEM_LIMIT)


def cost(microseconds):
    flops = int(microseconds * 1.1e9)
    return pl.CostEstimate(flops=flops, bytes_accessed=10**6, transcendentals=0)


def in_vmem():
    return pl.BlockSpec(memory_space=pltpu.VMEM)


def in_hbm():
    return pl.BlockSpec(memory_space=pltpu.HBM)


def in_smem():
    return pl.BlockSpec(memory_space=pltpu.SMEM)


def window_start(part, parts):
    return jnp.clip((part - 1) * NB, 0, (parts - 3) * NB)


def packed(count):
    return jax.ShapeDtypeStruct((count * W + count * W // 8, 256), BF16)


def pack_own_kernel(p_ref, out_ref):
    out_ref[0:ROWS, :] = p_ref[:, 0:256]
    for g in range(NB // 16):
        tails = [p_ref[48 * (8 * g + q) : 48 * (8 * g + q) + 48, 256:288] for q in range(8)]
        out_ref[ROWS + 48 * g : ROWS + 48 * g + 48, :] = jnp.concatenate(tails, axis=1)


def pack_rows(wide_ref, row_of, out_ref):
    for g in range(NS // 16):
        tails = []
        for q in range(8):
            t = 8 * g + q
            two = [wide_ref[row_of(2 * t + odd)] for odd in range(2)]
            pair = jnp.concatenate(two, axis=0).astype(BF16)
            out_ref[48 * t : 48 * t + 48, :] = pair[:, 0:256]
            tails.append(pair[:, 256:288])
        start = NS * W + 48 * g
        out_ref[start : start + 48, :] = jnp.concatenate(tails, axis=1)


def packed_pairs(packed_ref, g):
    tail_rows = pl.ds(pl.multiple_of(ROWS + g * 48, 48), 48)
    tails = [packed_ref[tail_rows, 128 * h : 128 * h + 128].astype(F32) for h in range(2)]
    for q in range(8):
        rows = pl.ds(pl.multiple_of((8 * g + q) * 48, 48), 48)
        x0, x1 = [packed_ref[rows, 128 * h : 128 * h + 128].astype(F32) for h in range(2)]
        shift = (-32 * (q % 4)) % 128
        tail = tails[q // 4]
        yield q, x0, x1, pltpu.roll(tail, shift, 1) if shift else tail


def widen(packed_ref, wide_ref):
    def group(g, carry):
        for q, x0, x1, tail in packed_pairs(packed_ref, g):
            for odd in range(2):
                r, rows = 2 * (8 * g + q) + odd, slice(24 * odd, 24 * odd + 24)
                wide_ref[r, :, 0:128] = x0[rows]
                wide_ref[r, :, 128:256] = x1[rows]
                wide_ref[r, :, 256:288] = tail[rows, 0:32]
        return carry

    lax.fori_loop(0, NB // 16, group, 0)


def pack_halo_kernel(place_ref, halo_ref, p_ref, down_ref, up_ref, wide_ref):
    part = place_ref[0]
    widen(p_ref, wide_ref)
    pack_rows(wide_ref, lambda n: halo_ref[part, 1, n], up_ref)
    pack_rows(wide_ref, lambda n: halo_ref[part, 0, n], down_ref)


def prepare_kernel(place_ref, aggs_ref, live_ref, p_ref, a_ref, spread_ref, blocks_ref, wide_ref, *, parts):
    part, col = place_ref[0], place_ref[1]
    own = part * NB - window_start(part, parts)
    lane = lax.broadcasted_iota(I32, (48, 128), 1)
    wide_ref[...] = jnp.zeros_like(wide_ref)
    to = lax.broadcasted_iota(I32, (256, 128), 1)
    come = W * jnp.bitwise_xor(to // W, col) + to % W
    at = lax.broadcasted_iota(I32, (256, 128), 0)

    def one_hot(shift):
        return jnp.logical_and(at == come + shift, to < BW).astype(F32).astype(BF16)

    for k in range(KA):
        start = BW * k // 128 * 128
        stop = min(start + 256, KA * BW)
        pick = one_hot(BW * k - start)[0 : stop - start]
        for n in range(3):
            rows = slice(512 * n, 512 * n + 512)
            got = jnp.dot(a_ref[rows, start:stop], pick, preferred_element_type=F32)
            blocks_ref[k, rows, :] = got.astype(BF16)

    def group(g, carry):
        for q, x0, x1, tail in packed_pairs(p_ref, g):
            blocks = (
                x0,
                jnp.where(lane < 32, pltpu.roll(x0, 32, 1), pltpu.roll(x1, 32, 1)),
                jnp.where(lane < 64, pltpu.roll(x1, 64, 1), pltpu.roll(tail, 64, 1)),
            )
            for odd in range(2):
                r = 2 * (8 * g + q) + odd
                live = (r < live_ref[0]).astype(F32)
                for m in range(KP):
                    block = aggs_ref[KP * (own + r) + m] - part * NAG
                    after = block // NAG
                    turn = jnp.bitwise_xor(block - NAG * after, col)
                    place = 2 * (3 - (2 * (turn % 2) + turn // 2)) + after
                    value = jnp.where(lane < 96, blocks[m], 0.0)[24 * odd : 24 * odd + 24] * live
                    wide_ref[place, pl.ds(pl.multiple_of(r * W, 8), W), :] = value
        return carry

    lax.fori_loop(0, NB // 16, group, 0)
    eye = (
        lax.broadcasted_iota(I32, (BC, 128), 0) == lax.broadcasted_iota(I32, (BC, 128), 1)
    ).astype(F32).astype(BF16)
    for b in range(8):
        for n in range(3):
            flipped = lax.dot_general(
                eye,
                wide_ref[b, 512 * n : 512 * n + 512, :].astype(BF16),
                (((1,), (1,)), ((), ())),
                preferred_element_type=F32,
            )
            spread_ref[BC * b : BC * b + BC, 512 * n : 512 * n + 512] = flipped.astype(BF16)


def unpack(count, sources, prolong):
    lane = lax.broadcasted_iota(I32, (48, 128), 1)

    def group(g, carry):
        tails = []
        for source in sources:
            rows = pl.ds(pl.multiple_of(count * W + g * 48, 48), 48)
            tails.append([source[rows, 128 * h : 128 * h + 128].astype(F32) for h in range(2)])
        for q in range(8):
            t = 8 * g + q
            parts = [[], [], []]
            for v, source in enumerate(sources):
                rows = pl.ds(pl.multiple_of(t * 48, 48), 48)
                x0 = source[rows, 0:128].astype(F32)
                x1 = source[rows, 128:256].astype(F32)
                tail, shift = tails[v][q // 4], (64 - 32 * (q % 4)) % 128
                if shift:
                    tail = pltpu.roll(tail, shift, 1)
                parts[0].append(x0)
                parts[1].append(jnp.where(lane < 32, pltpu.roll(x0, 32, 1), pltpu.roll(x1, 32, 1)))
                parts[2].append(jnp.where(lane < 64, pltpu.roll(x1, 64, 1), tail))
            for j in range(KP):
                for odd in range(2):
                    rows = [x[24 * odd : 24 * odd + 24] for x in parts[j]]
                    block = jnp.concatenate(rows, axis=0).astype(BF16)
                    prolong[2 * t + odd, :, 128 * j : 128 * j + 128] = block
        return carry

    lax.fori_loop(0, count // 16, group, 0)


def add_products(step, slots, a_ref, first_slot, prolong, row_of, blocks_of, sums):
    for slot in slots:
        for u in range(UN):
            i = UN * step + u
            odd = u % 2
            start = pl.multiple_of(step * (UN * W) + 48 * (u // 2) + 16 * odd, 16)
            at = row_of(i, slot)
            got = jnp.dot(
                a_ref[slot - first_slot, pl.ds(start, 32), 0:BW], prolong[at[0]], preferred_element_type=F32
            )[8 * odd : 8 * odd + 24]
            where = blocks_of(at[1])
            held = [sums[u][step, c] for c in where]
            for j in range(KP):
                sums[u][step, where[j]] = held[j] + got[:, 128 * j : 128 * j + 128]


def own_kernel(place_ref, aggs_ref, cols_ref, *refs, parts):
    part = place_ref[0]
    a_hbm, sums, (prolong, a_ref, sem) = refs[4], refs[5 : 5 + UN], refs[5 + UN :]
    a_copy = pltpu.make_async_copy(a_hbm, a_ref, sem)
    a_copy.start()
    unpack(NB, refs[0:4], prolong)
    a_copy.wait()
    own = part * NB - window_start(part, parts)
    base = part * NAG

    def row_of(i, slot):
        row = cols_ref[KA * i + slot]
        if slot < 5:
            row = row - part * NB
        return row, row

    def blocks_of(row):
        return [aggs_ref[KP * (own + row) + j] - base for j in range(KP)]

    def run(slots, fresh):
        def step(n, carry):
            if fresh:
                for each in sums:
                    each[n] = jnp.zeros((8, W, 128), F32)
            add_products(n, slots, a_ref, 0, prolong, row_of, blocks_of, sums)
            return carry

        lax.fori_loop(0, STEPS, step, 0, unroll=2 if fresh else 1)

    run((0, 1, 2, 3, 4), True)

    @pl.when(part == 0)
    def _():
        run((5, 6), False)

    @pl.when(part == parts - 1)
    def _():
        run((7, 8), False)


def halo_kernel(place_ref, halo_ref, aggs_ref, cols_ref, *refs, parts, upper):
    sources, a_hbm, own, coupled = refs[0:4], refs[4], refs[5:9], refs[9]
    prolong, a_ref, sums, sem = refs[10], refs[11], refs[12:16], refs[16]
    part = place_ref[0]
    slots = (7, 8) if upper else (5, 6)
    other = jnp.minimum(part + 1, parts - 1) if upper else jnp.maximum(part - 1, 0)
    rows_at = other * NB - window_start(part, parts)
    inside = part < parts - 1 if upper else part > 0
    a_copy = pltpu.make_async_copy(a_hbm.at[slots[0] : slots[0] + 2], a_ref, sem)
    a_copy.start()

    @pl.when(inside)
    def _():
        unpack(NS, sources, prolong)

    a_copy.wait()

    lane = lax.broadcasted_iota(I32, (48, 128), 1)

    def row_of(i, slot):
        at = cols_ref[KA * i + slot]
        return at, rows_at + halo_ref[other, 0 if upper else 1, at]

    def blocks_of(row):
        return [aggs_ref[KP * row + j] - other * NAG for j in range(KP)]

    def sum_of(n, u, c):
        if upper:
            return sums[u][n, c] + own[u][n, NAG + c] if c < NAG else sums[u][n, c]
        return sums[u][n, c] + own[u][n, c - NAG] if c >= NAG else sums[u][n, c]

    def run(products):
        def step(n, carry):
            for each in sums:
                each[n] = jnp.zeros((8, W, 128), F32)
            if products:
                add_products(n, slots, a_ref, slots[0], prolong, row_of, blocks_of, sums)
            for two in range(2):
                rows = pl.ds(pl.multiple_of(n * (UN * W) + 48 * two, 48), 48)
                for half in range(2):
                    y0, y1, y2, y3 = [
                        jnp.concatenate([sum_of(n, 2 * two, c), sum_of(n, 2 * two + 1, c)], axis=0)
                        for c in range(4 * half, 4 * half + 4)
                    ]
                    y1, y2, y3 = pltpu.roll(y1, 96, 1), pltpu.roll(y2, 64, 1), pltpu.roll(y3, 32, 1)
                    tiles = [
                        jnp.where(lane < 96, y0, y1),
                        jnp.where(lane < 64, y1, y2),
                        jnp.where(lane < 32, y2, y3),
                    ]
                    for x in range(3):
                        at = 384 * half + 128 * x
                        coupled[rows, at : at + 128] = tiles[x].astype(BF16)
            return carry

        lax.fori_loop(0, STEPS, step, 0, unroll=2 if products else 1)

    @pl.when(inside)
    def _():
        run(True)

    @pl.when(jnp.logical_not(inside))
    def _():
        run(False)


def coarse_kernel(spread, coupled, out_ref, *, half):
    for n in range(3):
        at = slice(256 * n, 256 * n + 256)
        got = jnp.dot(
            spread[384 * half : 384 * half + 384, :], coupled[:, at], preferred_element_type=F32
        )
        out_ref[:, at] = got.astype(out_ref.dtype)


def local(a_vals, p_vals, a_cols, p_aggs, halo_rows, live_rows):
    part = lax.axis_index("dom")
    parts = lax.axis_size("dom")
    col = lax.axis_index("col")
    cols_count = lax.axis_size("col")
    devices = [(d, c) for d in range(parts) for c in range(cols_count)]

    def moved(x, step, flip):
        route = [
            (d * cols_count + c, (d + step) * cols_count + (c ^ flip))
            for d, c in devices
            if 0 <= d + step < parts
        ]
        return lax.ppermute(x, AXES, route)

    place = jnp.stack([part, col]).astype(I32)
    p_flat = p_vals.reshape(ROWS, KP * BC)
    a_flat = a_vals.reshape(ROWS, KA * BW)
    wide = pltpu.VMEM((NB, W, KP * BC), F32)
    own_pack = pl.pallas_call(
        pack_own_kernel,
        out_shape=packed(NB),
        in_specs=[in_vmem()],
        out_specs=in_vmem(),
        compiler_params=params(),
        cost_estimate=cost(2),
    )(p_flat)
    near = moved(own_pack, 0, 2)
    down, upward = pl.pallas_call(
        pack_halo_kernel,
        out_shape=[packed(NS)] * 2,
        in_specs=[in_smem(), in_smem(), in_vmem()],
        out_specs=[in_vmem()] * 2,
        scratch_shapes=[wide],
        compiler_params=params(),
        cost_estimate=cost(3),
    )(place, halo_rows, own_pack)
    low = moved(upward, 1, 0)
    up = moved(down, -1, 0)

    def both_cores(x, far):
        return (x, moved(x, 0, 1), far, moved(far, 0, 1))

    aggs = lax.dynamic_slice_in_dim(p_aggs, window_start(part, parts), 3 * NB, 0).reshape(3 * NB * KP)
    cols = a_cols.reshape(NB * KA)
    spread, blocks = pl.pallas_call(
        lambda *refs: prepare_kernel(*refs, parts=parts),
        out_shape=[
            jax.ShapeDtypeStruct((8 * BC, ROWS), BF16),
            jax.ShapeDtypeStruct((KA, ROWS, 128), BF16),
        ],
        in_specs=[in_smem()] * 3 + [in_vmem()] * 2,
        out_specs=[in_vmem()] * 2,
        scratch_shapes=[pltpu.VMEM((8, ROWS, 128), F32)],
        compiler_params=params(),
        cost_estimate=cost(9),
    )(place, aggs, live_rows, own_pack, a_flat)
    near, low, spread = lax.optimization_barrier((near, low, spread))
    low_far = moved(low, 0, 2)

    sums_type = jax.ShapeDtypeStruct((STEPS, 8, W, 128), F32)
    own = pl.pallas_call(
        lambda *refs: own_kernel(*refs, parts=parts),
        out_shape=[sums_type] * UN,
        in_specs=[in_smem()] * 3 + [in_vmem()] * 4 + [in_hbm()],
        out_specs=[in_vmem()] * UN,
        scratch_shapes=[
            pltpu.VMEM((NB, BW, KP * 128), BF16),
            pltpu.VMEM((KA, ROWS, 128), BF16),
            pltpu.SemaphoreType.DMA,
        ],
        compiler_params=params(),
        cost_estimate=cost(10),
    )(place, aggs, cols, *both_cores(own_pack, near), blocks)
    up, low_far, first_sums = lax.optimization_barrier((up, low_far, own[0]))
    own = (first_sums, *own[1:])
    up_far = moved(up, 0, 2)

    def coupled_of(upper, sources):
        return pl.pallas_call(
            lambda *refs: halo_kernel(*refs, parts=parts, upper=upper),
            out_shape=jax.ShapeDtypeStruct((ROWS, 8 * BC), BF16),
            in_specs=[in_smem()] * 4 + [in_vmem()] * 4 + [in_hbm()] + [in_vmem()] * UN,
            out_specs=in_vmem(),
            scratch_shapes=[
                pltpu.VMEM((NS, BW, KP * 128), BF16),
                pltpu.VMEM((2, ROWS, 128), BF16),
                *[pltpu.VMEM((STEPS, 8, W, 128), F32)] * UN,
                pltpu.SemaphoreType.DMA,
            ],
            compiler_params=params(),
            cost_estimate=cost(6),
        )(place, halo_rows, aggs, cols, *sources, blocks, *own)

    def coarse_of(coupled, half):
        return pl.pallas_call(
            lambda *refs: coarse_kernel(*refs, half=half),
            out_shape=jax.ShapeDtypeStruct((4 * BC, 8 * BC), F32 if half else BF16),
            in_specs=[in_vmem()] * 2,
            out_specs=in_vmem(),
            compiler_params=params(),
            cost_estimate=cost(1.5),
        )(spread, coupled)

    low_coupled = coupled_of(False, both_cores(low, low_far))
    low_coupled, up_far = lax.optimization_barrier((low_coupled, up_far))
    low_came = moved(coarse_of(low_coupled, 0), 0, 1)
    low_keep = coarse_of(low_coupled, 1)
    up_sources = both_cores(up, up_far)
    low_both = low_keep + low_came.astype(F32)
    low_away = low_both[: 2 * BC].astype(BF16)
    up_coupled = coupled_of(True, up_sources)
    low_away, up_coupled = lax.optimization_barrier((low_away, up_coupled))
    low_far_next = moved(low_away[BC:], 0, 2)
    low_next = (low_both[3 * BC :] + low_far_next.astype(F32)).astype(BF16)
    up_came = moved(coarse_of(up_coupled, 0), 0, 1)
    up_keep = coarse_of(up_coupled, 1)
    low_next, up_keep = lax.optimization_barrier((low_next, up_keep))
    up_both = up_keep + up_came.astype(F32)
    away = up_both.astype(BF16)
    near_next = moved(jnp.concatenate([low_next, away[3 * BC :]], axis=0), 1, 0)
    far_next = moved(away[BC : 2 * BC], 1, 2)
    far_own = moved(jnp.concatenate([low_away[:BC], away[0:BC]], axis=0), 0, 2)
    near_next, far_next, far_own = lax.optimization_barrier((near_next, far_next, far_own))
    far_own = far_own.astype(F32)
    low_own, low_next = low_both[2 * BC : 3 * BC] + far_own[:BC], near_next[:BC].astype(F32)
    up_own = up_both[2 * BC : 3 * BC] + far_own[BC:]
    up_next = near_next[BC:].astype(F32) + far_next.astype(F32)
    band = NAG * BC
    mine = jnp.concatenate([low_own, up_own], axis=1)
    came = jnp.concatenate([low_next, up_next], axis=1)
    result = jnp.pad(mine, ((0, 0), (band, 0))) + jnp.pad(came, ((0, 0), (0, band)))
    return result.astype(BF16)


def solution(mesh):
    in_specs = (P("dom", "col", None), P("dom", "col", None), P("dom", None), P(), P(), P("dom"))
    out_specs = P(("dom", "col"), None)
    return jax.shard_map(local, mesh=mesh, in_specs=in_specs, out_specs=out_specs, check_vma=False)
```

```python
import jax
import jax.numpy as jnp
from jax import lax
from jax.experimental import pallas as pl
from jax.experimental.pallas import tpu as pltpu
from jax.sharding import PartitionSpec as P

BW = 96
BC = 96
KA = 9
KP = 3
NAG = 4
NB = 64
NS = 32
W = 24
ROWS = NB * W
UN = 4
STEPS = NB // UN
AXES = ("dom", "col")
VMEM_LIMIT = 16 * 1024 * 1024
F32, BF16, I32 = jnp.float32, jnp.bfloat16, jnp.int32


def params():
    return pltpu.CompilerParams(vmem_limit_bytes=VMEM_LIMIT)


def cost(microseconds):
    flops = int(microseconds * 1.1e9)
    return pl.CostEstimate(flops=flops, bytes_accessed=10**6, transcendentals=0)


def in_vmem():
    return pl.BlockSpec(memory_space=pltpu.VMEM)


def in_hbm():
    return pl.BlockSpec(memory_space=pltpu.HBM)


def in_smem():
    return pl.BlockSpec(memory_space=pltpu.SMEM)


def window_start(part, parts):
    return jnp.clip((part - 1) * NB, 0, (parts - 3) * NB)


def packed(count):
    return jax.ShapeDtypeStruct((count * W + count * W // 8, 256), BF16)


def pack_own_kernel(p_ref, out_ref):
    out_ref[0:ROWS, :] = p_ref[:, 0:256]
    for g in range(NB // 16):
        tails = [p_ref[48 * (8 * g + q) : 48 * (8 * g + q) + 48, 256:288] for q in range(8)]
        out_ref[ROWS + 48 * g : ROWS + 48 * g + 48, :] = jnp.concatenate(tails, axis=1)


def pack_rows(wide_ref, row_of, out_ref):
    for g in range(NS // 16):
        tails = []
        for q in range(8):
            t = 8 * g + q
            two = [wide_ref[row_of(2 * t + odd)] for odd in range(2)]
            pair = jnp.concatenate(two, axis=0).astype(BF16)
            out_ref[48 * t : 48 * t + 48, :] = pair[:, 0:256]
            tails.append(pair[:, 256:288])
        start = NS * W + 48 * g
        out_ref[start : start + 48, :] = jnp.concatenate(tails, axis=1)


def packed_pairs(packed_ref, g):
    tail_rows = pl.ds(pl.multiple_of(ROWS + g * 48, 48), 48)
    tails = [packed_ref[tail_rows, 128 * h : 128 * h + 128].astype(F32) for h in range(2)]
    for q in range(8):
        rows = pl.ds(pl.multiple_of((8 * g + q) * 48, 48), 48)
        x0, x1 = [packed_ref[rows, 128 * h : 128 * h + 128].astype(F32) for h in range(2)]
        shift = (-32 * (q % 4)) % 128
        tail = tails[q // 4]
        yield q, x0, x1, pltpu.roll(tail, shift, 1) if shift else tail


def widen(packed_ref, wide_ref):
    def group(g, carry):
        for q, x0, x1, tail in packed_pairs(packed_ref, g):
            for odd in range(2):
                r, rows = 2 * (8 * g + q) + odd, slice(24 * odd, 24 * odd + 24)
                wide_ref[r, :, 0:128] = x0[rows]
                wide_ref[r, :, 128:256] = x1[rows]
                wide_ref[r, :, 256:288] = tail[rows, 0:32]
        return carry

    lax.fori_loop(0, NB // 16, group, 0)


def pack_halo_kernel(place_ref, halo_ref, p_ref, down_ref, up_ref, wide_ref):
    part = place_ref[0]
    widen(p_ref, wide_ref)
    pack_rows(wide_ref, lambda n: halo_ref[part, 1, n], up_ref)
    pack_rows(wide_ref, lambda n: halo_ref[part, 0, n], down_ref)


def prepare_kernel(place_ref, aggs_ref, live_ref, p_ref, a_ref, spread_ref, blocks_ref, wide_ref, *, parts):
    part, col = place_ref[0], place_ref[1]
    own = part * NB - window_start(part, parts)
    lane = lax.broadcasted_iota(I32, (48, 128), 1)
    wide_ref[...] = jnp.zeros_like(wide_ref)
    to = lax.broadcasted_iota(I32, (256, 128), 1)
    come = W * jnp.bitwise_xor(to // W, col) + to % W
    at = lax.broadcasted_iota(I32, (256, 128), 0)

    def one_hot(shift):
        return jnp.logical_and(at == come + shift, to < BW).astype(F32).astype(BF16)

    for k in range(KA):
        start = BW * k // 128 * 128
        stop = min(start + 256, KA * BW)
        pick = one_hot(BW * k - start)[0 : stop - start]
        for n in range(3):
            rows = slice(512 * n, 512 * n + 512)
            got = jnp.dot(a_ref[rows, start:stop], pick, preferred_element_type=F32)
            blocks_ref[k, rows, :] = got.astype(BF16)

    def group(g, carry):
        for q, x0, x1, tail in packed_pairs(p_ref, g):
            blocks = (
                x0,
                jnp.where(lane < 32, pltpu.roll(x0, 32, 1), pltpu.roll(x1, 32, 1)),
                jnp.where(lane < 64, pltpu.roll(x1, 64, 1), pltpu.roll(tail, 64, 1)),
            )
            for odd in range(2):
                r = 2 * (8 * g + q) + odd
                live = (r < live_ref[0]).astype(F32)
                for m in range(KP):
                    block = aggs_ref[KP * (own + r) + m] - part * NAG
                    after = block // NAG
                    turn = jnp.bitwise_xor(block - NAG * after, col)
                    place = 2 * (3 - (2 * (turn % 2) + turn // 2)) + after
                    value = jnp.where(lane < 96, blocks[m], 0.0)[24 * odd : 24 * odd + 24] * live
                    wide_ref[place, pl.ds(pl.multiple_of(r * W, 8), W), :] = value
        return carry

    lax.fori_loop(0, NB // 16, group, 0)
    eye = (
        lax.broadcasted_iota(I32, (BC, 128), 0) == lax.broadcasted_iota(I32, (BC, 128), 1)
    ).astype(F32).astype(BF16)
    for b in range(8):
        for n in range(3):
            flipped = lax.dot_general(
                eye,
                wide_ref[b, 512 * n : 512 * n + 512, :].astype(BF16),
                (((1,), (1,)), ((), ())),
                preferred_element_type=F32,
            )
            spread_ref[BC * b : BC * b + BC, 512 * n : 512 * n + 512] = flipped.astype(BF16)


def unpack(count, sources, prolong):
    lane = lax.broadcasted_iota(I32, (48, 128), 1)

    def group(g, carry):
        tails = []
        for source in sources:
            rows = pl.ds(pl.multiple_of(count * W + g * 48, 48), 48)
            tails.append([source[rows, 128 * h : 128 * h + 128].astype(F32) for h in range(2)])
        for q in range(8):
            t = 8 * g + q
            parts = [[], [], []]
            for v, source in enumerate(sources):
                rows = pl.ds(pl.multiple_of(t * 48, 48), 48)
                x0 = source[rows, 0:128].astype(F32)
                x1 = source[rows, 128:256].astype(F32)
                tail, shift = tails[v][q // 4], (64 - 32 * (q % 4)) % 128
                if shift:
                    tail = pltpu.roll(tail, shift, 1)
                parts[0].append(x0)
                parts[1].append(jnp.where(lane < 32, pltpu.roll(x0, 32, 1), pltpu.roll(x1, 32, 1)))
                parts[2].append(jnp.where(lane < 64, pltpu.roll(x1, 64, 1), tail))
            for j in range(KP):
                for odd in range(2):
                    rows = [x[24 * odd : 24 * odd + 24] for x in parts[j]]
                    block = jnp.concatenate(rows, axis=0).astype(BF16)
                    prolong[2 * t + odd, :, 128 * j : 128 * j + 128] = block
        return carry

    lax.fori_loop(0, count // 16, group, 0)


def add_products(step, slots, a_ref, first_slot, prolong, row_of, blocks_of, sums):
    for slot in slots:
        for u in range(UN):
            i = UN * step + u
            odd = u % 2
            start = pl.multiple_of(step * (UN * W) + 48 * (u // 2) + 16 * odd, 16)
            at = row_of(i, slot)
            got = jnp.dot(
                a_ref[slot - first_slot, pl.ds(start, 32), 0:BW], prolong[at[0]], preferred_element_type=F32
            )[8 * odd : 8 * odd + 24]
            where = blocks_of(at[1])
            held = [sums[u][step, c] for c in where]
            for j in range(KP):
                sums[u][step, where[j]] = held[j] + got[:, 128 * j : 128 * j + 128]


def own_rows(part, parts, cols_ref, aggs_ref):
    own = part * NB - window_start(part, parts)

    def row_of(i, slot):
        row = cols_ref[KA * i + slot]
        if slot < 5:
            row = row - part * NB
        return row, row

    def blocks_of(row):
        return [aggs_ref[KP * (own + row) + j] - part * NAG for j in range(KP)]

    return row_of, blocks_of


def own_kernel(place_ref, aggs_ref, cols_ref, *refs, parts):
    part = place_ref[0]
    a_hbm, prolong, sums, (a_ref, sem) = refs[4], refs[5], refs[6 : 6 + UN], refs[6 + UN :]
    a_copy = pltpu.make_async_copy(a_hbm, a_ref, sem)
    a_copy.start()
    unpack(NB, refs[0:4], prolong)
    a_copy.wait()
    row_of, blocks_of = own_rows(part, parts, cols_ref, aggs_ref)

    def step(n, carry):
        for each in sums:
            each[n] = jnp.zeros((8, W, 128), F32)
        add_products(n, range(5), a_ref, 0, prolong, row_of, blocks_of, sums)
        return carry

    lax.fori_loop(0, STEPS, step, 0, unroll=4)


def halo_rows_of(part, parts, upper, halo_ref, cols_ref, aggs_ref):
    other = jnp.minimum(part + 1, parts - 1) if upper else jnp.maximum(part - 1, 0)
    rows_at = other * NB - window_start(part, parts)

    def row_of(i, slot):
        at = cols_ref[KA * i + slot]
        return at, rows_at + halo_ref[other, 0 if upper else 1, at]

    def blocks_of(row):
        return [aggs_ref[KP * row + j] - other * NAG for j in range(KP)]

    return row_of, blocks_of


def couple(n, block_of, coupled):
    lane = lax.broadcasted_iota(I32, (48, 128), 1)
    for two in range(2):
        rows = pl.ds(pl.multiple_of(n * (UN * W) + 48 * two, 48), 48)
        for half in range(2):
            y0, y1, y2, y3 = [
                jnp.concatenate([block_of(2 * two, c), block_of(2 * two + 1, c)], axis=0)
                for c in range(4 * half, 4 * half + 4)
            ]
            y1, y2, y3 = pltpu.roll(y1, 96, 1), pltpu.roll(y2, 64, 1), pltpu.roll(y3, 32, 1)
            tiles = [
                jnp.where(lane < 96, y0, y1),
                jnp.where(lane < 64, y1, y2),
                jnp.where(lane < 32, y2, y3),
            ]
            for x in range(3):
                at = 384 * half + 128 * x
                coupled[rows, at : at + 128] = tiles[x].astype(BF16)


def lower_kernel(place_ref, halo_ref, aggs_ref, cols_ref, *refs, parts):
    sources, a_hbm, own_hbm, own, coupled, above = refs[0:4], refs[4], refs[5], refs[6:10], refs[10], refs[11:15]
    prolong, a_ref, sums, sem, own_sem = refs[15], refs[16], refs[17:21], refs[21], refs[22]
    part = place_ref[0]
    a_copy = pltpu.make_async_copy(a_hbm.at[5:9], a_ref, sem)
    a_copy.start()
    own_row, own_block = own_rows(part, parts, cols_ref, aggs_ref)
    row_of, blocks_of = halo_rows_of(part, parts, False, halo_ref, cols_ref, aggs_ref)

    def swapped(row):
        return [jnp.bitwise_xor(c, NAG) for c in own_block(row)]

    def clear(n):
        for each in sums:
            each[n] = jnp.zeros((8, W, 128), F32)

    def fetch_own():
        copy = pltpu.make_async_copy(own_hbm, prolong, own_sem)
        copy.start()
        copy.wait()

    def finish(n):
        couple(n, lambda u, c: sums[u][n, c] + own[u][n, c - NAG] if c >= NAG else sums[u][n, c], coupled)
        for u in range(UN):
            above[u][n] = own[u][n, NAG : 2 * NAG]

    @pl.when(part == parts - 1)
    def _():
        fetch_own()
        a_copy.wait()

        def step(n, carry):
            clear(n)
            add_products(n, (7, 8), a_ref, 5, prolong, own_row, swapped, sums)
            return carry

        lax.fori_loop(0, STEPS, step, 0, unroll=2)
        unpack(NS, sources, prolong)

        def step(n, carry):
            add_products(n, (5, 6), a_ref, 5, prolong, row_of, blocks_of, sums)
            finish(n)
            return carry

        lax.fori_loop(0, STEPS, step, 0, unroll=2)

    @pl.when(part == 0)
    def _():
        fetch_own()
        a_copy.wait()

        def step(n, carry):
            clear(n)
            add_products(n, (5, 6), a_ref, 5, prolong, own_row, swapped, sums)
            nothing = jnp.zeros((W, 128), F32)
            couple(n, lambda u, c: sums[u][n, c] + own[u][n, c - NAG] if c >= NAG else nothing, coupled)
            for u in range(UN):
                above[u][n] = own[u][n, NAG : 2 * NAG] + sums[u][n, 0:NAG]
            return carry

        lax.fori_loop(0, STEPS, step, 0, unroll=2)

    @pl.when(jnp.logical_and(part > 0, part < parts - 1))
    def _():
        unpack(NS, sources, prolong)
        a_copy.wait()

        def step(n, carry):
            clear(n)
            add_products(n, (5, 6), a_ref, 5, prolong, row_of, blocks_of, sums)
            finish(n)
            return carry

        lax.fori_loop(0, STEPS, step, 0, unroll=2)


def upper_kernel(place_ref, halo_ref, aggs_ref, cols_ref, *refs, parts):
    sources, a_hbm, above, coupled = refs[0:4], refs[4], refs[5:9], refs[9]
    prolong, a_ref, sums, sem = refs[10], refs[11], refs[12:16], refs[16]
    part = place_ref[0]
    a_copy = pltpu.make_async_copy(a_hbm.at[7:9], a_ref, sem)
    a_copy.start()
    row_of, blocks_of = halo_rows_of(part, parts, True, halo_ref, cols_ref, aggs_ref)
    inside = part < parts - 1

    @pl.when(inside)
    def _():
        unpack(NS, sources, prolong)

    a_copy.wait()

    def run(products):
        def step(n, carry):
            for each in sums:
                each[n] = jnp.zeros((8, W, 128), F32)
            if products:
                add_products(n, (7, 8), a_ref, 7, prolong, row_of, blocks_of, sums)
            couple(n, lambda u, c: sums[u][n, c] + above[u][n, c] if c < NAG else sums[u][n, c], coupled)
            return carry

        lax.fori_loop(0, STEPS, step, 0, unroll=2 if products else 1)

    @pl.when(inside)
    def _():
        run(True)

    @pl.when(jnp.logical_not(inside))
    def _():
        run(False)


def coarse_kernel(spread, coupled, out_ref, *, half):
    for n in range(3):
        at = slice(256 * n, 256 * n + 256)
        got = jnp.dot(
            spread[384 * half : 384 * half + 384, :], coupled[:, at], preferred_element_type=F32
        )
        out_ref[:, at] = got.astype(out_ref.dtype)


def local(a_vals, p_vals, a_cols, p_aggs, halo_rows, live_rows):
    part = lax.axis_index("dom")
    parts = lax.axis_size("dom")
    col = lax.axis_index("col")
    cols_count = lax.axis_size("col")
    devices = [(d, c) for d in range(parts) for c in range(cols_count)]

    def moved(x, step, flip):
        route = [
            (d * cols_count + c, (d + step) * cols_count + (c ^ flip))
            for d, c in devices
            if 0 <= d + step < parts
        ]
        return lax.ppermute(x, AXES, route)

    place = jnp.stack([part, col]).astype(I32)
    p_flat = p_vals.reshape(ROWS, KP * BC)
    a_flat = a_vals.reshape(ROWS, KA * BW)
    wide = pltpu.VMEM((NB, W, KP * BC), F32)
    own_pack = pl.pallas_call(
        pack_own_kernel,
        out_shape=packed(NB),
        in_specs=[in_vmem()],
        out_specs=in_vmem(),
        compiler_params=params(),
        cost_estimate=cost(2),
    )(p_flat)
    near = moved(own_pack, 0, 2)
    down, upward = pl.pallas_call(
        pack_halo_kernel,
        out_shape=[packed(NS)] * 2,
        in_specs=[in_smem(), in_smem(), in_vmem()],
        out_specs=[in_vmem()] * 2,
        scratch_shapes=[wide],
        compiler_params=params(),
        cost_estimate=cost(3),
    )(place, halo_rows, own_pack)
    low = moved(upward, 1, 0)
    up = moved(down, -1, 0)

    def both_cores(x, far):
        return (x, moved(x, 0, 1), far, moved(far, 0, 1))

    aggs = lax.dynamic_slice_in_dim(p_aggs, window_start(part, parts), 3 * NB, 0).reshape(3 * NB * KP)
    cols = a_cols.reshape(NB * KA)
    spread, blocks = pl.pallas_call(
        lambda *refs: prepare_kernel(*refs, parts=parts),
        out_shape=[
            jax.ShapeDtypeStruct((8 * BC, ROWS), BF16),
            jax.ShapeDtypeStruct((KA, ROWS, 128), BF16),
        ],
        in_specs=[in_smem()] * 3 + [in_vmem()] * 2,
        out_specs=[in_vmem()] * 2,
        scratch_shapes=[pltpu.VMEM((8, ROWS, 128), F32)],
        compiler_params=params(),
        cost_estimate=cost(9),
    )(place, aggs, live_rows, own_pack, a_flat)
    near, low, spread = lax.optimization_barrier((near, low, spread))
    low_far = moved(low, 0, 2)

    sums_type = jax.ShapeDtypeStruct((STEPS, 8, W, 128), F32)
    prolong_type = jax.ShapeDtypeStruct((NB, BW, KP * 128), BF16)
    prolong, *own = pl.pallas_call(
        lambda *refs: own_kernel(*refs, parts=parts),
        out_shape=[prolong_type] + [sums_type] * UN,
        in_specs=[in_smem()] * 3 + [in_vmem()] * 4 + [in_hbm()],
        out_specs=[in_vmem()] * (1 + UN),
        scratch_shapes=[pltpu.VMEM((KA, ROWS, 128), BF16), pltpu.SemaphoreType.DMA],
        compiler_params=params(),
        cost_estimate=cost(10),
    )(place, aggs, cols, *both_cores(own_pack, near), blocks)
    up, low_far, first_sums = lax.optimization_barrier((up, low_far, own[0]))
    own = (first_sums, *own[1:])
    up_far = moved(up, 0, 2)
    coupled_type = jax.ShapeDtypeStruct((ROWS, 8 * BC), BF16)
    above_type = jax.ShapeDtypeStruct((STEPS, NAG, W, 128), F32)
    sums_scratch = [pltpu.VMEM((STEPS, 8, W, 128), F32)] * UN
    low_coupled, *above = pl.pallas_call(
        lambda *refs: lower_kernel(*refs, parts=parts),
        out_shape=[coupled_type] + [above_type] * UN,
        in_specs=[in_smem()] * 4 + [in_vmem()] * 4 + [in_hbm()] * 2 + [in_vmem()] * UN,
        out_specs=[in_vmem()] * (1 + UN),
        scratch_shapes=[
            pltpu.VMEM((NB, BW, KP * 128), BF16),
            pltpu.VMEM((4, ROWS, 128), BF16),
            *sums_scratch,
            pltpu.SemaphoreType.DMA,
            pltpu.SemaphoreType.DMA,
        ],
        compiler_params=params(),
        cost_estimate=cost(6),
    )(place, halo_rows, aggs, cols, *both_cores(low, low_far), blocks, prolong, *own)

    def upper_coupled(sources, above):
        return pl.pallas_call(
            lambda *refs: upper_kernel(*refs, parts=parts),
            out_shape=coupled_type,
            in_specs=[in_smem()] * 4 + [in_vmem()] * 4 + [in_hbm()] + [in_vmem()] * UN,
            out_specs=in_vmem(),
            scratch_shapes=[
                pltpu.VMEM((NS, BW, KP * 128), BF16),
                pltpu.VMEM((2, ROWS, 128), BF16),
                *sums_scratch,
                pltpu.SemaphoreType.DMA,
            ],
            compiler_params=params(),
            cost_estimate=cost(6),
        )(place, halo_rows, aggs, cols, *sources, blocks, *above)

    def coarse_of(coupled, half, weight):
        return pl.pallas_call(
            lambda *refs: coarse_kernel(*refs, half=half),
            out_shape=jax.ShapeDtypeStruct((4 * BC, 8 * BC), F32 if half else BF16),
            in_specs=[in_vmem()] * 2,
            out_specs=in_vmem(),
            compiler_params=params(),
            cost_estimate=cost(weight),
        )(spread, coupled)

    low_came = moved(coarse_of(low_coupled, 0, 0.01), 0, 1)
    low_keep = coarse_of(low_coupled, 1, 0.01)
    low_keep, up_far = lax.optimization_barrier((low_keep, up_far))
    *up_sources, last_source = both_cores(up, up_far)
    low_came, last_source = lax.optimization_barrier((low_came, last_source))
    up_sources = (*up_sources, last_source)
    low_both = low_keep + low_came.astype(F32)
    low_away = low_both[: 2 * BC].astype(BF16)
    low_away, first_above = lax.optimization_barrier((low_away, above[0]))
    low_far_next = moved(low_away[BC:], 0, 2)
    up_coupled = upper_coupled(up_sources, (first_above, *above[1:]))
    low_far_next, up_coupled = lax.optimization_barrier((low_far_next, up_coupled))
    low_next = (low_both[3 * BC :] + low_far_next.astype(F32)).astype(BF16)
    up_came = moved(coarse_of(up_coupled, 0, 1.5), 0, 1)
    up_keep = coarse_of(up_coupled, 1, 1.5)
    up_both = up_keep + up_came.astype(F32)
    away = up_both.astype(BF16)
    near_next = moved(jnp.concatenate([low_next, away[3 * BC :]], axis=0), 1, 0)
    far_next = moved(away[BC : 2 * BC], 1, 2)
    far_own = moved(jnp.concatenate([low_away[:BC], away[0:BC]], axis=0), 0, 2)
    near_next, far_next, far_own = lax.optimization_barrier((near_next, far_next, far_own))
    far_own = far_own.astype(F32)
    low_own, low_next = low_both[2 * BC : 3 * BC] + far_own[:BC], near_next[:BC].astype(F32)
    up_own = up_both[2 * BC : 3 * BC] + far_own[BC:]
    up_next = near_next[BC:].astype(F32) + far_next.astype(F32)
    band = NAG * BC
    mine = jnp.concatenate([low_own, up_own], axis=1)
    came = jnp.concatenate([low_next, up_next], axis=1)
    result = jnp.pad(mine, ((0, 0), (band, 0))) + jnp.pad(came, ((0, 0), (0, band)))
    return result.astype(BF16)


def solution(mesh):
    in_specs = (P("dom", "col", None), P("dom", "col", None), P("dom", None), P(), P(), P("dom"))
    out_specs = P(("dom", "col"), None)
    return jax.shard_map(local, mesh=mesh, in_specs=in_specs, out_specs=out_specs, check_vma=False)
```

```python
import jax
import jax.numpy as jnp
from jax import lax
from jax.experimental import pallas as pl
from jax.experimental.pallas import tpu as pltpu
from jax.sharding import PartitionSpec as P

BW = 96
BC = 96
KA = 9
KP = 3
NAG = 4
NB = 64
NS = 32
W = 24
ROWS = NB * W
UN = 4
STEPS = NB // UN
AXES = ("dom", "col")
VMEM_LIMIT = 16 * 1024 * 1024
F32, BF16, I32 = jnp.float32, jnp.bfloat16, jnp.int32


def params():
    return pltpu.CompilerParams(vmem_limit_bytes=VMEM_LIMIT)


def cost(microseconds):
    flops = int(microseconds * 1.1e9)
    return pl.CostEstimate(flops=flops, bytes_accessed=10**6, transcendentals=0)


def in_vmem():
    return pl.BlockSpec(memory_space=pltpu.VMEM)


def in_hbm():
    return pl.BlockSpec(memory_space=pltpu.HBM)


def in_smem():
    return pl.BlockSpec(memory_space=pltpu.SMEM)


def window_start(part, parts):
    return jnp.clip((part - 1) * NB, 0, (parts - 3) * NB)


def packed(count):
    return jax.ShapeDtypeStruct((count * W + count * W // 8, 256), BF16)


def pack_own_kernel(p_ref, out_ref):
    out_ref[0:ROWS, :] = p_ref[:, 0:256]
    for g in range(NB // 16):
        tails = [p_ref[48 * (8 * g + q) : 48 * (8 * g + q) + 48, 256:288] for q in range(8)]
        out_ref[ROWS + 48 * g : ROWS + 48 * g + 48, :] = jnp.concatenate(tails, axis=1)


def pack_rows(wide_ref, row_of, out_ref):
    for g in range(NS // 16):
        tails = []
        for q in range(8):
            t = 8 * g + q
            two = [wide_ref[row_of(2 * t + odd)] for odd in range(2)]
            pair = jnp.concatenate(two, axis=0).astype(BF16)
            out_ref[48 * t : 48 * t + 48, :] = pair[:, 0:256]
            tails.append(pair[:, 256:288])
        start = NS * W + 48 * g
        out_ref[start : start + 48, :] = jnp.concatenate(tails, axis=1)


def packed_pairs(packed_ref, g):
    tail_rows = pl.ds(pl.multiple_of(ROWS + g * 48, 48), 48)
    tails = [packed_ref[tail_rows, 128 * h : 128 * h + 128].astype(F32) for h in range(2)]
    for q in range(8):
        rows = pl.ds(pl.multiple_of((8 * g + q) * 48, 48), 48)
        x0, x1 = [packed_ref[rows, 128 * h : 128 * h + 128].astype(F32) for h in range(2)]
        shift = (-32 * (q % 4)) % 128
        tail = tails[q // 4]
        yield q, x0, x1, pltpu.roll(tail, shift, 1) if shift else tail


def widen(packed_ref, wide_ref):
    def group(g, carry):
        for q, x0, x1, tail in packed_pairs(packed_ref, g):
            for odd in range(2):
                r, rows = 2 * (8 * g + q) + odd, slice(24 * odd, 24 * odd + 24)
                wide_ref[r, :, 0:128] = x0[rows]
                wide_ref[r, :, 128:256] = x1[rows]
                wide_ref[r, :, 256:288] = tail[rows, 0:32]
        return carry

    lax.fori_loop(0, NB // 16, group, 0)


def pack_halo_kernel(place_ref, halo_ref, p_ref, down_ref, up_ref, wide_ref):
    part = place_ref[0]
    widen(p_ref, wide_ref)
    pack_rows(wide_ref, lambda n: halo_ref[part, 1, n], up_ref)
    pack_rows(wide_ref, lambda n: halo_ref[part, 0, n], down_ref)


def prepare_kernel(place_ref, aggs_ref, live_ref, p_ref, a_ref, spread_ref, blocks_ref, wide_ref, *, parts):
    part, col = place_ref[0], place_ref[1]
    own = part * NB - window_start(part, parts)
    lane = lax.broadcasted_iota(I32, (48, 128), 1)
    wide_ref[...] = jnp.zeros_like(wide_ref)
    to = lax.broadcasted_iota(I32, (256, 128), 1)
    come = W * jnp.bitwise_xor(to // W, col) + to % W
    at = lax.broadcasted_iota(I32, (256, 128), 0)

    def one_hot(shift):
        return jnp.logical_and(at == come + shift, to < BW).astype(F32).astype(BF16)

    for k in range(KA):
        start = BW * k // 128 * 128
        stop = min(start + 256, KA * BW)
        pick = one_hot(BW * k - start)[0 : stop - start]
        for n in range(3):
            rows = slice(512 * n, 512 * n + 512)
            got = jnp.dot(a_ref[rows, start:stop], pick, preferred_element_type=F32)
            blocks_ref[k, rows, :] = got.astype(BF16)

    def group(g, carry):
        for q, x0, x1, tail in packed_pairs(p_ref, g):
            blocks = (
                x0,
                jnp.where(lane < 32, pltpu.roll(x0, 32, 1), pltpu.roll(x1, 32, 1)),
                jnp.where(lane < 64, pltpu.roll(x1, 64, 1), pltpu.roll(tail, 64, 1)),
            )
            for odd in range(2):
                r = 2 * (8 * g + q) + odd
                live = (r < live_ref[0]).astype(F32)
                for m in range(KP):
                    block = aggs_ref[KP * (own + r) + m] - part * NAG
                    after = block // NAG
                    turn = jnp.bitwise_xor(block - NAG * after, col)
                    place = 2 * (3 - (2 * (turn % 2) + turn // 2)) + after
                    value = jnp.where(lane < 96, blocks[m], 0.0)[24 * odd : 24 * odd + 24] * live
                    wide_ref[place, pl.ds(pl.multiple_of(r * W, 8), W), :] = value
        return carry

    lax.fori_loop(0, NB // 16, group, 0)
    eye = (
        lax.broadcasted_iota(I32, (BC, 128), 0) == lax.broadcasted_iota(I32, (BC, 128), 1)
    ).astype(F32).astype(BF16)
    for b in range(8):
        for n in range(3):
            flipped = lax.dot_general(
                eye,
                wide_ref[b, 512 * n : 512 * n + 512, :].astype(BF16),
                (((1,), (1,)), ((), ())),
                preferred_element_type=F32,
            )
            spread_ref[BC * b : BC * b + BC, 512 * n : 512 * n + 512] = flipped.astype(BF16)


def unpack(count, sources, prolong):
    lane = lax.broadcasted_iota(I32, (48, 128), 1)

    def group(g, carry):
        tails = []
        for source in sources:
            rows = pl.ds(pl.multiple_of(count * W + g * 48, 48), 48)
            tails.append([source[rows, 128 * h : 128 * h + 128].astype(F32) for h in range(2)])
        for q in range(8):
            t = 8 * g + q
            parts = [[], [], []]
            for v, source in enumerate(sources):
                rows = pl.ds(pl.multiple_of(t * 48, 48), 48)
                x0 = source[rows, 0:128].astype(F32)
                x1 = source[rows, 128:256].astype(F32)
                tail, shift = tails[v][q // 4], (64 - 32 * (q % 4)) % 128
                if shift:
                    tail = pltpu.roll(tail, shift, 1)
                parts[0].append(x0)
                parts[1].append(jnp.where(lane < 32, pltpu.roll(x0, 32, 1), pltpu.roll(x1, 32, 1)))
                parts[2].append(jnp.where(lane < 64, pltpu.roll(x1, 64, 1), tail))
            for j in range(KP):
                for odd in range(2):
                    rows = [x[24 * odd : 24 * odd + 24] for x in parts[j]]
                    block = jnp.concatenate(rows, axis=0).astype(BF16)
                    prolong[2 * t + odd, :, 128 * j : 128 * j + 128] = block
        return carry

    lax.fori_loop(0, count // 16, group, 0)


def add_products(step, slots, a_ref, first_slot, prolong, row_of, blocks_of, sums):
    for slot in slots:
        for u in range(UN):
            i = UN * step + u
            odd = u % 2
            start = pl.multiple_of(step * (UN * W) + 48 * (u // 2) + 16 * odd, 16)
            at = row_of(i, slot)
            got = jnp.dot(
                a_ref[slot - first_slot, pl.ds(start, 32), 0:BW], prolong[at[0]], preferred_element_type=F32
            )[8 * odd : 8 * odd + 24]
            where = blocks_of(at[1])
            held = [sums[u][step, c] for c in where]
            for j in range(KP):
                sums[u][step, where[j]] = held[j] + got[:, 128 * j : 128 * j + 128]


def own_rows(part, parts, cols_ref, aggs_ref):
    own = part * NB - window_start(part, parts)

    def row_of(i, slot):
        row = cols_ref[KA * i + slot]
        if slot < 5:
            row = row - part * NB
        return row, row

    def blocks_of(row):
        return [aggs_ref[KP * (own + row) + j] - part * NAG for j in range(KP)]

    return row_of, blocks_of


def own_kernel(place_ref, aggs_ref, cols_ref, *refs, parts):
    part = place_ref[0]
    a_hbm, prolong, sums, (a_ref, sem) = refs[4], refs[5], refs[6 : 6 + UN], refs[6 + UN :]
    a_copy = pltpu.make_async_copy(a_hbm, a_ref, sem)
    a_copy.start()
    unpack(NB, refs[0:4], prolong)
    a_copy.wait()
    row_of, blocks_of = own_rows(part, parts, cols_ref, aggs_ref)

    def step(n, carry):
        for each in sums:
            each[n] = jnp.zeros((8, W, 128), F32)
        add_products(n, range(5), a_ref, 0, prolong, row_of, blocks_of, sums)
        return carry

    lax.fori_loop(0, STEPS, step, 0, unroll=4)


def halo_rows_of(part, parts, upper, halo_ref, cols_ref, aggs_ref):
    other = jnp.minimum(part + 1, parts - 1) if upper else jnp.maximum(part - 1, 0)
    rows_at = other * NB - window_start(part, parts)

    def row_of(i, slot):
        at = cols_ref[KA * i + slot]
        return at, rows_at + halo_ref[other, 0 if upper else 1, at]

    def blocks_of(row):
        return [aggs_ref[KP * row + j] - other * NAG for j in range(KP)]

    return row_of, blocks_of


def couple(n, block_of, coupled):
    lane = lax.broadcasted_iota(I32, (48, 128), 1)
    for two in range(2):
        rows = pl.ds(pl.multiple_of(n * (UN * W) + 48 * two, 48), 48)
        for half in range(2):
            y0, y1, y2, y3 = [
                jnp.concatenate([block_of(2 * two, c), block_of(2 * two + 1, c)], axis=0)
                for c in range(4 * half, 4 * half + 4)
            ]
            y1, y2, y3 = pltpu.roll(y1, 96, 1), pltpu.roll(y2, 64, 1), pltpu.roll(y3, 32, 1)
            tiles = [
                jnp.where(lane < 96, y0, y1),
                jnp.where(lane < 64, y1, y2),
                jnp.where(lane < 32, y2, y3),
            ]
            for x in range(3):
                at = 384 * half + 128 * x
                coupled[rows, at : at + 128] = tiles[x].astype(BF16)


def lower_kernel(place_ref, halo_ref, aggs_ref, cols_ref, *refs, parts):
    sources, a_hbm, own_hbm, own, coupled, above = refs[0:4], refs[4], refs[5], refs[6:10], refs[10], refs[11:15]
    prolong, a_ref, sums, sem, own_sem = refs[15], refs[16], refs[17:21], refs[21], refs[22]
    part = place_ref[0]
    a_copy = pltpu.make_async_copy(a_hbm.at[5:9], a_ref, sem)
    a_copy.start()
    own_row, own_block = own_rows(part, parts, cols_ref, aggs_ref)
    row_of, blocks_of = halo_rows_of(part, parts, False, halo_ref, cols_ref, aggs_ref)

    def swapped(row):
        return [jnp.bitwise_xor(c, NAG) for c in own_block(row)]

    def clear(n):
        for each in sums:
            each[n] = jnp.zeros((8, W, 128), F32)

    def fetch_own():
        copy = pltpu.make_async_copy(own_hbm, prolong, own_sem)
        copy.start()
        copy.wait()

    def finish(n):
        couple(n, lambda u, c: sums[u][n, c] + own[u][n, c - NAG] if c >= NAG else sums[u][n, c], coupled)
        for u in range(UN):
            above[u][n] = own[u][n, NAG : 2 * NAG]

    @pl.when(part == parts - 1)
    def _():
        fetch_own()
        a_copy.wait()

        def step(n, carry):
            clear(n)
            add_products(n, (7, 8), a_ref, 5, prolong, own_row, swapped, sums)
            return carry

        lax.fori_loop(0, STEPS, step, 0, unroll=4)
        unpack(NS, sources, prolong)

        def step(n, carry):
            add_products(n, (5, 6), a_ref, 5, prolong, row_of, blocks_of, sums)
            finish(n)
            return carry

        lax.fori_loop(0, STEPS, step, 0, unroll=4)

    @pl.when(part == 0)
    def _():
        fetch_own()
        a_copy.wait()

        def step(n, carry):
            clear(n)
            add_products(n, (5, 6), a_ref, 5, prolong, own_row, swapped, sums)
            nothing = jnp.zeros((W, 128), F32)
            couple(n, lambda u, c: sums[u][n, c] + own[u][n, c - NAG] if c >= NAG else nothing, coupled)
            for u in range(UN):
                above[u][n] = own[u][n, NAG : 2 * NAG] + sums[u][n, 0:NAG]
            return carry

        lax.fori_loop(0, STEPS, step, 0, unroll=4)

    @pl.when(jnp.logical_and(part > 0, part < parts - 1))
    def _():
        unpack(NS, sources, prolong)
        a_copy.wait()

        def step(n, carry):
            clear(n)
            add_products(n, (5, 6), a_ref, 5, prolong, row_of, blocks_of, sums)
            finish(n)
            return carry

        lax.fori_loop(0, STEPS, step, 0, unroll=4)


def upper_kernel(place_ref, halo_ref, aggs_ref, cols_ref, *refs, parts):
    sources, a_hbm, above, coupled = refs[0:4], refs[4], refs[5:9], refs[9]
    prolong, a_ref, sums, sem = refs[10], refs[11], refs[12:16], refs[16]
    part = place_ref[0]
    a_copy = pltpu.make_async_copy(a_hbm.at[7:9], a_ref, sem)
    a_copy.start()
    row_of, blocks_of = halo_rows_of(part, parts, True, halo_ref, cols_ref, aggs_ref)
    inside = part < parts - 1

    @pl.when(inside)
    def _():
        unpack(NS, sources, prolong)

    a_copy.wait()

    def run(products):
        def step(n, carry):
            for each in sums:
                each[n] = jnp.zeros((8, W, 128), F32)
            if products:
                add_products(n, (7, 8), a_ref, 7, prolong, row_of, blocks_of, sums)
            couple(n, lambda u, c: sums[u][n, c] + above[u][n, c] if c < NAG else sums[u][n, c], coupled)
            return carry

        lax.fori_loop(0, STEPS, step, 0, unroll=4 if products else 1)

    @pl.when(inside)
    def _():
        run(True)

    @pl.when(jnp.logical_not(inside))
    def _():
        run(False)


def coarse_kernel(spread, coupled, out_ref, *, half):
    for n in range(3):
        at = slice(256 * n, 256 * n + 256)
        got = jnp.dot(
            spread[384 * half : 384 * half + 384, :], coupled[:, at], preferred_element_type=F32
        )
        out_ref[:, at] = got.astype(out_ref.dtype)


def local(a_vals, p_vals, a_cols, p_aggs, halo_rows, live_rows):
    part = lax.axis_index("dom")
    parts = lax.axis_size("dom")
    col = lax.axis_index("col")
    cols_count = lax.axis_size("col")
    devices = [(d, c) for d in range(parts) for c in range(cols_count)]

    def moved(x, step, flip):
        route = [
            (d * cols_count + c, (d + step) * cols_count + (c ^ flip))
            for d, c in devices
            if 0 <= d + step < parts
        ]
        return lax.ppermute(x, AXES, route)

    place = jnp.stack([part, col]).astype(I32)
    p_flat = p_vals.reshape(ROWS, KP * BC)
    a_flat = a_vals.reshape(ROWS, KA * BW)
    wide = pltpu.VMEM((NB, W, KP * BC), F32)
    own_pack = pl.pallas_call(
        pack_own_kernel,
        out_shape=packed(NB),
        in_specs=[in_vmem()],
        out_specs=in_vmem(),
        compiler_params=params(),
        cost_estimate=cost(2),
    )(p_flat)
    near = moved(own_pack, 0, 2)
    down, upward = pl.pallas_call(
        pack_halo_kernel,
        out_shape=[packed(NS)] * 2,
        in_specs=[in_smem(), in_smem(), in_vmem()],
        out_specs=[in_vmem()] * 2,
        scratch_shapes=[wide],
        compiler_params=params(),
        cost_estimate=cost(3),
    )(place, halo_rows, own_pack)
    low = moved(upward, 1, 0)

    def both_cores(x, far):
        return (x, moved(x, 0, 1), far, moved(far, 0, 1))

    aggs = lax.dynamic_slice_in_dim(p_aggs, window_start(part, parts), 3 * NB, 0).reshape(3 * NB * KP)
    cols = a_cols.reshape(NB * KA)
    spread, blocks = pl.pallas_call(
        lambda *refs: prepare_kernel(*refs, parts=parts),
        out_shape=[
            jax.ShapeDtypeStruct((8 * BC, ROWS), BF16),
            jax.ShapeDtypeStruct((KA, ROWS, 128), BF16),
        ],
        in_specs=[in_smem()] * 3 + [in_vmem()] * 2,
        out_specs=[in_vmem()] * 2,
        scratch_shapes=[pltpu.VMEM((8, ROWS, 128), F32)],
        compiler_params=params(),
        cost_estimate=cost(9),
    )(place, aggs, live_rows, own_pack, a_flat)
    down, low, spread = lax.optimization_barrier((down, low, spread))
    up = moved(down, -1, 0)
    near, spread = lax.optimization_barrier((near, spread))
    low_far = moved(low, 0, 2)

    sums_type = jax.ShapeDtypeStruct((STEPS, 8, W, 128), F32)
    prolong_type = jax.ShapeDtypeStruct((NB, BW, KP * 128), BF16)
    prolong, *own = pl.pallas_call(
        lambda *refs: own_kernel(*refs, parts=parts),
        out_shape=[prolong_type] + [sums_type] * UN,
        in_specs=[in_smem()] * 3 + [in_vmem()] * 4 + [in_hbm()],
        out_specs=[in_vmem()] * (1 + UN),
        scratch_shapes=[pltpu.VMEM((KA, ROWS, 128), BF16), pltpu.SemaphoreType.DMA],
        compiler_params=params(),
        cost_estimate=cost(10),
    )(place, aggs, cols, *both_cores(own_pack, near), blocks)
    up, low_far, first_sums = lax.optimization_barrier((up, low_far, own[0]))
    own = (first_sums, *own[1:])
    up_far = moved(up, 0, 2)
    coupled_type = jax.ShapeDtypeStruct((ROWS, 8 * BC), BF16)
    above_type = jax.ShapeDtypeStruct((STEPS, NAG, W, 128), F32)
    sums_scratch = [pltpu.VMEM((STEPS, 8, W, 128), F32)] * UN
    low_coupled, *above = pl.pallas_call(
        lambda *refs: lower_kernel(*refs, parts=parts),
        out_shape=[coupled_type] + [above_type] * UN,
        in_specs=[in_smem()] * 4 + [in_vmem()] * 4 + [in_hbm()] * 2 + [in_vmem()] * UN,
        out_specs=[in_vmem()] * (1 + UN),
        scratch_shapes=[
            pltpu.VMEM((NB, BW, KP * 128), BF16),
            pltpu.VMEM((4, ROWS, 128), BF16),
            *sums_scratch,
            pltpu.SemaphoreType.DMA,
            pltpu.SemaphoreType.DMA,
        ],
        compiler_params=params(),
        cost_estimate=cost(6),
    )(place, halo_rows, aggs, cols, *both_cores(low, low_far), blocks, prolong, *own)

    def upper_coupled(sources, above):
        return pl.pallas_call(
            lambda *refs: upper_kernel(*refs, parts=parts),
            out_shape=coupled_type,
            in_specs=[in_smem()] * 4 + [in_vmem()] * 4 + [in_hbm()] + [in_vmem()] * UN,
            out_specs=in_vmem(),
            scratch_shapes=[
                pltpu.VMEM((NS, BW, KP * 128), BF16),
                pltpu.VMEM((2, ROWS, 128), BF16),
                *sums_scratch,
                pltpu.SemaphoreType.DMA,
            ],
            compiler_params=params(),
            cost_estimate=cost(6),
        )(place, halo_rows, aggs, cols, *sources, blocks, *above)

    def coarse_of(coupled, half, weight):
        return pl.pallas_call(
            lambda *refs: coarse_kernel(*refs, half=half),
            out_shape=jax.ShapeDtypeStruct((4 * BC, 8 * BC), F32 if half else BF16),
            in_specs=[in_vmem()] * 2,
            out_specs=in_vmem(),
            compiler_params=params(),
            cost_estimate=cost(weight),
        )(spread, coupled)

    low_came = moved(coarse_of(low_coupled, 0, 0.01), 0, 1)
    low_keep = coarse_of(low_coupled, 1, 0.01)
    low_keep, up_far = lax.optimization_barrier((low_keep, up_far))
    *up_sources, last_source = both_cores(up, up_far)
    low_came, last_source = lax.optimization_barrier((low_came, last_source))
    up_sources = (*up_sources, last_source)
    low_both = low_keep + low_came.astype(F32)
    low_away = low_both[: 2 * BC].astype(BF16)
    low_away, first_above = lax.optimization_barrier((low_away, above[0]))
    low_far_next = moved(low_away[BC:], 0, 2)
    up_coupled = upper_coupled(up_sources, (first_above, *above[1:]))
    low_far_next, up_coupled = lax.optimization_barrier((low_far_next, up_coupled))
    low_next = (low_both[3 * BC :] + low_far_next.astype(F32)).astype(BF16)
    up_came = moved(coarse_of(up_coupled, 0, 1.5), 0, 1)
    up_keep = coarse_of(up_coupled, 1, 1.5)
    up_both = up_keep + up_came.astype(F32)
    away = up_both.astype(BF16)
    near_next = moved(jnp.concatenate([low_next, away[3 * BC :]], axis=0), 1, 0)
    far_next = moved(away[BC : 2 * BC], 1, 2)
    far_own = moved(jnp.concatenate([low_away[:BC], away[0:BC]], axis=0), 0, 2)
    near_next, far_next, far_own = lax.optimization_barrier((near_next, far_next, far_own))
    far_own = far_own.astype(F32)
    low_own, low_next = low_both[2 * BC : 3 * BC] + far_own[:BC], near_next[:BC].astype(F32)
    up_own = up_both[2 * BC : 3 * BC] + far_own[BC:]
    up_next = near_next[BC:].astype(F32) + far_next.astype(F32)
    band = NAG * BC
    mine = jnp.concatenate([low_own, up_own], axis=1)
    came = jnp.concatenate([low_next, up_next], axis=1)
    result = jnp.pad(mine, ((0, 0), (band, 0))) + jnp.pad(came, ((0, 0), (0, band)))
    return result.astype(BF16)


def solution(mesh):
    in_specs = (P("dom", "col", None), P("dom", "col", None), P("dom", None), P(), P(), P("dom"))
    out_specs = P(("dom", "col"), None)
    return jax.shard_map(local, mesh=mesh, in_specs=in_specs, out_specs=out_specs, check_vma=False)
```

```python
import jax
import jax.numpy as jnp
from jax import lax
from jax.experimental import pallas as pl
from jax.experimental.pallas import tpu as pltpu
from jax.sharding import PartitionSpec as P

BW = 96
BC = 96
KA = 9
KP = 3
NAG = 4
NB = 64
NS = 32
W = 24
ROWS = NB * W
UN = 4
STEPS = NB // UN
AXES = ("dom", "col")
VMEM_LIMIT = 16 * 1024 * 1024
F32, BF16, I32 = jnp.float32, jnp.bfloat16, jnp.int32


def params():
    return pltpu.CompilerParams(vmem_limit_bytes=VMEM_LIMIT)


def cost(microseconds):
    flops = int(microseconds * 1.1e9)
    return pl.CostEstimate(flops=flops, bytes_accessed=10**6, transcendentals=0)


def in_vmem():
    return pl.BlockSpec(memory_space=pltpu.VMEM)


def in_hbm():
    return pl.BlockSpec(memory_space=pltpu.HBM)


def in_smem():
    return pl.BlockSpec(memory_space=pltpu.SMEM)


def window_start(part, parts):
    return jnp.clip((part - 1) * NB, 0, (parts - 3) * NB)


def packed(count):
    return jax.ShapeDtypeStruct((count * W + count * W // 8, 256), BF16)


def pack_own_kernel(p_ref, out_ref):
    out_ref[0:ROWS, :] = p_ref[:, 0:256]
    for g in range(NB // 16):
        tails = [p_ref[48 * (8 * g + q) : 48 * (8 * g + q) + 48, 256:288] for q in range(8)]
        out_ref[ROWS + 48 * g : ROWS + 48 * g + 48, :] = jnp.concatenate(tails, axis=1)


def pack_rows(wide_ref, row_of, out_ref):
    for g in range(NS // 16):
        tails = []
        for q in range(8):
            t = 8 * g + q
            two = [wide_ref[row_of(2 * t + odd)] for odd in range(2)]
            pair = jnp.concatenate(two, axis=0).astype(BF16)
            out_ref[48 * t : 48 * t + 48, :] = pair[:, 0:256]
            tails.append(pair[:, 256:288])
        start = NS * W + 48 * g
        out_ref[start : start + 48, :] = jnp.concatenate(tails, axis=1)


def packed_pairs(packed_ref, g):
    tail_rows = pl.ds(pl.multiple_of(ROWS + g * 48, 48), 48)
    tails = [packed_ref[tail_rows, 128 * h : 128 * h + 128].astype(F32) for h in range(2)]
    for q in range(8):
        rows = pl.ds(pl.multiple_of((8 * g + q) * 48, 48), 48)
        x0, x1 = [packed_ref[rows, 128 * h : 128 * h + 128].astype(F32) for h in range(2)]
        shift = (-32 * (q % 4)) % 128
        tail = tails[q // 4]
        yield q, x0, x1, pltpu.roll(tail, shift, 1) if shift else tail


def widen(packed_ref, wide_ref):
    def group(g, carry):
        for q, x0, x1, tail in packed_pairs(packed_ref, g):
            for odd in range(2):
                r, rows = 2 * (8 * g + q) + odd, slice(24 * odd, 24 * odd + 24)
                wide_ref[r, :, 0:128] = x0[rows]
                wide_ref[r, :, 128:256] = x1[rows]
                wide_ref[r, :, 256:288] = tail[rows, 0:32]
        return carry

    lax.fori_loop(0, NB // 16, group, 0)


def pack_halo_kernel(place_ref, halo_ref, p_ref, down_ref, up_ref, wide_ref):
    part = place_ref[0]
    widen(p_ref, wide_ref)
    pack_rows(wide_ref, lambda n: halo_ref[part, 1, n], up_ref)
    pack_rows(wide_ref, lambda n: halo_ref[part, 0, n], down_ref)


def prepare_kernel(place_ref, aggs_ref, live_ref, p_ref, a_ref, spread_ref, blocks_ref, wide_ref, *, parts):
    part, col = place_ref[0], place_ref[1]
    own = part * NB - window_start(part, parts)
    lane = lax.broadcasted_iota(I32, (48, 128), 1)
    wide_ref[...] = jnp.zeros_like(wide_ref)
    to = lax.broadcasted_iota(I32, (256, 128), 1)
    come = W * jnp.bitwise_xor(to // W, col) + to % W
    at = lax.broadcasted_iota(I32, (256, 128), 0)

    def one_hot(shift):
        return jnp.logical_and(at == come + shift, to < BW).astype(F32).astype(BF16)

    for k in range(KA):
        start = BW * k // 128 * 128
        stop = min(start + 256, KA * BW)
        pick = one_hot(BW * k - start)[0 : stop - start]
        for n in range(3):
            rows = slice(512 * n, 512 * n + 512)
            got = jnp.dot(a_ref[rows, start:stop], pick, preferred_element_type=F32)
            blocks_ref[k, rows, :] = got.astype(BF16)

    def group(g, carry):
        for q, x0, x1, tail in packed_pairs(p_ref, g):
            blocks = (
                x0,
                jnp.where(lane < 32, pltpu.roll(x0, 32, 1), pltpu.roll(x1, 32, 1)),
                jnp.where(lane < 64, pltpu.roll(x1, 64, 1), pltpu.roll(tail, 64, 1)),
            )
            for odd in range(2):
                r = 2 * (8 * g + q) + odd
                live = (r < live_ref[0]).astype(F32)
                for m in range(KP):
                    block = aggs_ref[KP * (own + r) + m] - part * NAG
                    after = block // NAG
                    turn = jnp.bitwise_xor(block - NAG * after, col)
                    place = 2 * (3 - (2 * (turn % 2) + turn // 2)) + after
                    value = jnp.where(lane < 96, blocks[m], 0.0)[24 * odd : 24 * odd + 24] * live
                    wide_ref[place, pl.ds(pl.multiple_of(r * W, 8), W), :] = value
        return carry

    lax.fori_loop(0, NB // 16, group, 0)
    eye = (
        lax.broadcasted_iota(I32, (BC, 128), 0) == lax.broadcasted_iota(I32, (BC, 128), 1)
    ).astype(F32).astype(BF16)
    for b in range(8):
        for n in range(3):
            flipped = lax.dot_general(
                eye,
                wide_ref[b, 512 * n : 512 * n + 512, :].astype(BF16),
                (((1,), (1,)), ((), ())),
                preferred_element_type=F32,
            )
            spread_ref[BC * b : BC * b + BC, 512 * n : 512 * n + 512] = flipped.astype(BF16)


def unpack(count, sources, prolong):
    lane = lax.broadcasted_iota(I32, (48, 128), 1)

    def group(g, carry):
        tails = []
        for source in sources:
            rows = pl.ds(pl.multiple_of(count * W + g * 48, 48), 48)
            tails.append([source[rows, 128 * h : 128 * h + 128].astype(F32) for h in range(2)])
        for q in range(8):
            t = 8 * g + q
            parts = [[], [], []]
            for v, source in enumerate(sources):
                rows = pl.ds(pl.multiple_of(t * 48, 48), 48)
                x0 = source[rows, 0:128].astype(F32)
                x1 = source[rows, 128:256].astype(F32)
                tail, shift = tails[v][q // 4], (64 - 32 * (q % 4)) % 128
                if shift:
                    tail = pltpu.roll(tail, shift, 1)
                parts[0].append(x0)
                parts[1].append(jnp.where(lane < 32, pltpu.roll(x0, 32, 1), pltpu.roll(x1, 32, 1)))
                parts[2].append(jnp.where(lane < 64, pltpu.roll(x1, 64, 1), tail))
            for j in range(KP):
                for odd in range(2):
                    rows = [x[24 * odd : 24 * odd + 24] for x in parts[j]]
                    block = jnp.concatenate(rows, axis=0).astype(BF16)
                    prolong[2 * t + odd, :, 128 * j : 128 * j + 128] = block
        return carry

    lax.fori_loop(0, count // 16, group, 0)


def add_products(step, slots, a_ref, first_slot, prolong, row_of, blocks_of, sums):
    for slot in slots:
        for u in range(UN):
            i = UN * step + u
            odd = u % 2
            start = pl.multiple_of(step * (UN * W) + 48 * (u // 2) + 16 * odd, 16)
            at = row_of(i, slot)
            got = jnp.dot(
                a_ref[slot - first_slot, pl.ds(start, 32), 0:BW], prolong[at[0]], preferred_element_type=F32
            )[8 * odd : 8 * odd + 24]
            where = blocks_of(at[1])
            held = [sums[u][step, c] for c in where]
            for j in range(KP):
                sums[u][step, where[j]] = held[j] + got[:, 128 * j : 128 * j + 128]


def own_rows(part, parts, cols_ref, aggs_ref):
    own = part * NB - window_start(part, parts)

    def row_of(i, slot):
        row = cols_ref[KA * i + slot]
        if slot < 5:
            row = row - part * NB
        return row, row

    def blocks_of(row):
        return [aggs_ref[KP * (own + row) + j] - part * NAG for j in range(KP)]

    return row_of, blocks_of


def own_kernel(place_ref, aggs_ref, cols_ref, *refs, parts):
    part = place_ref[0]
    a_hbm, prolong, sums, (a_ref, sem) = refs[4], refs[5], refs[6 : 6 + UN], refs[6 + UN :]
    a_copy = pltpu.make_async_copy(a_hbm, a_ref, sem)
    a_copy.start()
    unpack(NB, refs[0:4], prolong)
    a_copy.wait()
    row_of, blocks_of = own_rows(part, parts, cols_ref, aggs_ref)

    def step(n, carry):
        for each in sums:
            each[n] = jnp.zeros((8, W, 128), F32)
        add_products(n, range(5), a_ref, 0, prolong, row_of, blocks_of, sums)
        return carry

    lax.fori_loop(0, STEPS, step, 0, unroll=8)


def halo_rows_of(part, parts, upper, halo_ref, cols_ref, aggs_ref):
    other = jnp.minimum(part + 1, parts - 1) if upper else jnp.maximum(part - 1, 0)
    rows_at = other * NB - window_start(part, parts)

    def row_of(i, slot):
        at = cols_ref[KA * i + slot]
        return at, rows_at + halo_ref[other, 0 if upper else 1, at]

    def blocks_of(row):
        return [aggs_ref[KP * row + j] - other * NAG for j in range(KP)]

    return row_of, blocks_of


def couple(n, block_of, coupled):
    lane = lax.broadcasted_iota(I32, (48, 128), 1)
    for two in range(2):
        rows = pl.ds(pl.multiple_of(n * (UN * W) + 48 * two, 48), 48)
        for half in range(2):
            y0, y1, y2, y3 = [
                jnp.concatenate([block_of(2 * two, c), block_of(2 * two + 1, c)], axis=0)
                for c in range(4 * half, 4 * half + 4)
            ]
            y1, y2, y3 = pltpu.roll(y1, 96, 1), pltpu.roll(y2, 64, 1), pltpu.roll(y3, 32, 1)
            tiles = [
                jnp.where(lane < 96, y0, y1),
                jnp.where(lane < 64, y1, y2),
                jnp.where(lane < 32, y2, y3),
            ]
            for x in range(3):
                at = 384 * half + 128 * x
                coupled[rows, at : at + 128] = tiles[x].astype(BF16)


def lower_kernel(place_ref, halo_ref, aggs_ref, cols_ref, *refs, parts):
    sources, a_hbm, own_hbm, own, coupled, above = refs[0:4], refs[4], refs[5], refs[6:10], refs[10], refs[11:15]
    prolong, a_ref, sums, sem, own_sem = refs[15], refs[16], refs[17:21], refs[21], refs[22]
    part = place_ref[0]
    a_copy = pltpu.make_async_copy(a_hbm.at[5:9], a_ref, sem)
    a_copy.start()
    own_row, own_block = own_rows(part, parts, cols_ref, aggs_ref)
    row_of, blocks_of = halo_rows_of(part, parts, False, halo_ref, cols_ref, aggs_ref)

    def swapped(row):
        return [jnp.bitwise_xor(c, NAG) for c in own_block(row)]

    def clear(n):
        for each in sums:
            each[n] = jnp.zeros((8, W, 128), F32)

    def fetch_own():
        copy = pltpu.make_async_copy(own_hbm, prolong, own_sem)
        copy.start()
        copy.wait()

    def finish(n):
        couple(n, lambda u, c: sums[u][n, c] + own[u][n, c - NAG] if c >= NAG else sums[u][n, c], coupled)
        for u in range(UN):
            above[u][n] = own[u][n, NAG : 2 * NAG]

    @pl.when(part == parts - 1)
    def _():
        fetch_own()
        a_copy.wait()

        def step(n, carry):
            clear(n)
            add_products(n, (7, 8), a_ref, 5, prolong, own_row, swapped, sums)
            return carry

        lax.fori_loop(0, STEPS, step, 0, unroll=4)
        unpack(NS, sources, prolong)

        def step(n, carry):
            add_products(n, (5, 6), a_ref, 5, prolong, row_of, blocks_of, sums)
            finish(n)
            return carry

        lax.fori_loop(0, STEPS, step, 0, unroll=4)

    @pl.when(part == 0)
    def _():
        fetch_own()
        a_copy.wait()

        def step(n, carry):
            clear(n)
            add_products(n, (5, 6), a_ref, 5, prolong, own_row, swapped, sums)
            nothing = jnp.zeros((W, 128), F32)
            couple(n, lambda u, c: sums[u][n, c] + own[u][n, c - NAG] if c >= NAG else nothing, coupled)
            for u in range(UN):
                above[u][n] = own[u][n, NAG : 2 * NAG] + sums[u][n, 0:NAG]
            return carry

        lax.fori_loop(0, STEPS, step, 0, unroll=4)

    @pl.when(jnp.logical_and(part > 0, part < parts - 1))
    def _():
        unpack(NS, sources, prolong)
        a_copy.wait()

        def step(n, carry):
            clear(n)
            add_products(n, (5, 6), a_ref, 5, prolong, row_of, blocks_of, sums)
            finish(n)
            return carry

        lax.fori_loop(0, STEPS, step, 0, unroll=4)


def upper_kernel(place_ref, halo_ref, aggs_ref, cols_ref, *refs, parts):
    sources, a_hbm, above, coupled = refs[0:4], refs[4], refs[5:9], refs[9]
    prolong, a_ref, sums, sem = refs[10], refs[11], refs[12:16], refs[16]
    part = place_ref[0]
    a_copy = pltpu.make_async_copy(a_hbm.at[7:9], a_ref, sem)
    a_copy.start()
    row_of, blocks_of = halo_rows_of(part, parts, True, halo_ref, cols_ref, aggs_ref)
    inside = part < parts - 1

    @pl.when(inside)
    def _():
        unpack(NS, sources, prolong)

    a_copy.wait()

    def run(products):
        def step(n, carry):
            for each in sums:
                each[n] = jnp.zeros((8, W, 128), F32)
            if products:
                add_products(n, (7, 8), a_ref, 7, prolong, row_of, blocks_of, sums)
            couple(n, lambda u, c: sums[u][n, c] + above[u][n, c] if c < NAG else sums[u][n, c], coupled)
            return carry

        lax.fori_loop(0, STEPS, step, 0, unroll=8 if products else 1)

    @pl.when(inside)
    def _():
        run(True)

    @pl.when(jnp.logical_not(inside))
    def _():
        run(False)


def coarse_kernel(spread, coupled, out_ref, *, half):
    for n in range(3):
        at = slice(256 * n, 256 * n + 256)
        got = jnp.dot(
            spread[384 * half : 384 * half + 384, :], coupled[:, at], preferred_element_type=F32
        )
        out_ref[:, at] = got.astype(out_ref.dtype)


def local(a_vals, p_vals, a_cols, p_aggs, halo_rows, live_rows):
    part = lax.axis_index("dom")
    parts = lax.axis_size("dom")
    col = lax.axis_index("col")
    cols_count = lax.axis_size("col")
    devices = [(d, c) for d in range(parts) for c in range(cols_count)]

    def moved(x, step, flip):
        route = [
            (d * cols_count + c, (d + step) * cols_count + (c ^ flip))
            for d, c in devices
            if 0 <= d + step < parts
        ]
        return lax.ppermute(x, AXES, route)

    place = jnp.stack([part, col]).astype(I32)
    p_flat = p_vals.reshape(ROWS, KP * BC)
    a_flat = a_vals.reshape(ROWS, KA * BW)
    wide = pltpu.VMEM((NB, W, KP * BC), F32)
    own_pack = pl.pallas_call(
        pack_own_kernel,
        out_shape=packed(NB),
        in_specs=[in_vmem()],
        out_specs=in_vmem(),
        compiler_params=params(),
        cost_estimate=cost(2),
    )(p_flat)
    near = moved(own_pack, 0, 2)
    down, upward = pl.pallas_call(
        pack_halo_kernel,
        out_shape=[packed(NS)] * 2,
        in_specs=[in_smem(), in_smem(), in_vmem()],
        out_specs=[in_vmem()] * 2,
        scratch_shapes=[wide],
        compiler_params=params(),
        cost_estimate=cost(3),
    )(place, halo_rows, own_pack)
    low = moved(upward, 1, 0)

    def both_cores(x, far):
        return (x, moved(x, 0, 1), far, moved(far, 0, 1))

    aggs = lax.dynamic_slice_in_dim(p_aggs, window_start(part, parts), 3 * NB, 0).reshape(3 * NB * KP)
    cols = a_cols.reshape(NB * KA)
    spread, blocks = pl.pallas_call(
        lambda *refs: prepare_kernel(*refs, parts=parts),
        out_shape=[
            jax.ShapeDtypeStruct((8 * BC, ROWS), BF16),
            jax.ShapeDtypeStruct((KA, ROWS, 128), BF16),
        ],
        in_specs=[in_smem()] * 3 + [in_vmem()] * 2,
        out_specs=[in_vmem()] * 2,
        scratch_shapes=[pltpu.VMEM((8, ROWS, 128), F32)],
        compiler_params=params(),
        cost_estimate=cost(9),
    )(place, aggs, live_rows, own_pack, a_flat)
    down, low, spread = lax.optimization_barrier((down, low, spread))
    up = moved(down, -1, 0)
    near, spread = lax.optimization_barrier((near, spread))
    low_far = moved(low, 0, 2)

    sums_type = jax.ShapeDtypeStruct((STEPS, 8, W, 128), F32)
    prolong_type = jax.ShapeDtypeStruct((NB, BW, KP * 128), BF16)
    prolong, *own = pl.pallas_call(
        lambda *refs: own_kernel(*refs, parts=parts),
        out_shape=[prolong_type] + [sums_type] * UN,
        in_specs=[in_smem()] * 3 + [in_vmem()] * 4 + [in_hbm()],
        out_specs=[in_vmem()] * (1 + UN),
        scratch_shapes=[pltpu.VMEM((KA, ROWS, 128), BF16), pltpu.SemaphoreType.DMA],
        compiler_params=params(),
        cost_estimate=cost(10),
    )(place, aggs, cols, *both_cores(own_pack, near), blocks)
    up, low_far, first_sums = lax.optimization_barrier((up, low_far, own[0]))
    own = (first_sums, *own[1:])
    up_far = moved(up, 0, 2)
    coupled_type = jax.ShapeDtypeStruct((ROWS, 8 * BC), BF16)
    above_type = jax.ShapeDtypeStruct((STEPS, NAG, W, 128), F32)
    sums_scratch = [pltpu.VMEM((STEPS, 8, W, 128), F32)] * UN
    low_coupled, *above = pl.pallas_call(
        lambda *refs: lower_kernel(*refs, parts=parts),
        out_shape=[coupled_type] + [above_type] * UN,
        in_specs=[in_smem()] * 4 + [in_vmem()] * 4 + [in_hbm()] * 2 + [in_vmem()] * UN,
        out_specs=[in_vmem()] * (1 + UN),
        scratch_shapes=[
            pltpu.VMEM((NB, BW, KP * 128), BF16),
            pltpu.VMEM((4, ROWS, 128), BF16),
            *sums_scratch,
            pltpu.SemaphoreType.DMA,
            pltpu.SemaphoreType.DMA,
        ],
        compiler_params=params(),
        cost_estimate=cost(6),
    )(place, halo_rows, aggs, cols, *both_cores(low, low_far), blocks, prolong, *own)

    def upper_coupled(sources, above):
        return pl.pallas_call(
            lambda *refs: upper_kernel(*refs, parts=parts),
            out_shape=coupled_type,
            in_specs=[in_smem()] * 4 + [in_vmem()] * 4 + [in_hbm()] + [in_vmem()] * UN,
            out_specs=in_vmem(),
            scratch_shapes=[
                pltpu.VMEM((NS, BW, KP * 128), BF16),
                pltpu.VMEM((2, ROWS, 128), BF16),
                *sums_scratch,
                pltpu.SemaphoreType.DMA,
            ],
            compiler_params=params(),
            cost_estimate=cost(6),
        )(place, halo_rows, aggs, cols, *sources, blocks, *above)

    def coarse_of(coupled, half, weight):
        return pl.pallas_call(
            lambda *refs: coarse_kernel(*refs, half=half),
            out_shape=jax.ShapeDtypeStruct((4 * BC, 8 * BC), F32 if half else BF16),
            in_specs=[in_vmem()] * 2,
            out_specs=in_vmem(),
            compiler_params=params(),
            cost_estimate=cost(weight),
        )(spread, coupled)

    low_came = moved(coarse_of(low_coupled, 0, 0.01), 0, 1)
    low_keep = coarse_of(low_coupled, 1, 0.01)
    low_keep, up_far = lax.optimization_barrier((low_keep, up_far))
    *up_sources, last_source = both_cores(up, up_far)
    low_came, last_source = lax.optimization_barrier((low_came, last_source))
    up_sources = (*up_sources, last_source)
    low_both = low_keep + low_came.astype(F32)
    low_away = low_both[: 2 * BC].astype(BF16)
    low_away, first_above = lax.optimization_barrier((low_away, above[0]))
    low_far_next = moved(low_away[BC:], 0, 2)
    up_coupled = upper_coupled(up_sources, (first_above, *above[1:]))
    low_far_next, up_coupled = lax.optimization_barrier((low_far_next, up_coupled))
    low_next = (low_both[3 * BC :] + low_far_next.astype(F32)).astype(BF16)
    up_came = moved(coarse_of(up_coupled, 0, 1.5), 0, 1)
    up_keep = coarse_of(up_coupled, 1, 1.5)
    up_both = up_keep + up_came.astype(F32)
    away = up_both.astype(BF16)
    near_next = moved(jnp.concatenate([low_next, away[3 * BC :]], axis=0), 1, 0)
    far_next = moved(away[BC : 2 * BC], 1, 2)
    far_own = moved(jnp.concatenate([low_away[:BC], away[0:BC]], axis=0), 0, 2)
    near_next, far_next, far_own = lax.optimization_barrier((near_next, far_next, far_own))
    far_own = far_own.astype(F32)
    low_own, low_next = low_both[2 * BC : 3 * BC] + far_own[:BC], near_next[:BC].astype(F32)
    up_own = up_both[2 * BC : 3 * BC] + far_own[BC:]
    up_next = near_next[BC:].astype(F32) + far_next.astype(F32)
    band = NAG * BC
    mine = jnp.concatenate([low_own, up_own], axis=1)
    came = jnp.concatenate([low_next, up_next], axis=1)
    result = jnp.pad(mine, ((0, 0), (band, 0))) + jnp.pad(came, ((0, 0), (0, band)))
    return result.astype(BF16)


def solution(mesh):
    in_specs = (P("dom", "col", None), P("dom", "col", None), P("dom", None), P(), P(), P("dom"))
    out_specs = P(("dom", "col"), None)
    return jax.shard_map(local, mesh=mesh, in_specs=in_specs, out_specs=out_specs, check_vma=False)
```
